512 devices in a mesh: clip: 32 (over y_lo, z, core), src: 16 (over x, y_hi).
Axes of the slice: x: 4, y: 8 (y_hi: 4, y_lo: 2; y = y_hi * 2 + y_lo), z: 8, core: 2. Of those that a mesh axis runs over, the one named last changes fastest.
Arguments:
- mask_field: float32 [64, 512, 512], P('clip'), may hold values from -6 to 6
- dose_code: int32 [64, 8, 512, 512], P('clip', None, 'src'), may hold values from 0 to 15
- target: float32 [64, 512, 512], P('clip', 'src'), may hold values from 0 to 1
- pupil: float32 [2, 64, 64], replicated, may hold values from -4 to 4
- source_index: int32 [32], P('src'), may hold values from 0 to 10200, as said below
- source_weight: float32 [32], P('src'), may hold values from 0.015625 to 0.0625
- tile_count: int32 [16], replicated, may hold values from 1 to 4
Outputs:
- grad_mask: float32 [64, 512, 512], P('clip', 'src')
- grad_source: float32 [32], P('src')
The draws below stay inside these ranges and needn't reach their ends.
Inputs may be any that keep to these rules, and one draw needn't show every extreme that they name: `source_index`: distinct points of the 101 x 101 grid, numbered row by row.
All inputs are finite; a program needn't handle non-finite values.
Results may differ from the reference program's by a relative error of at most 0.0003.
Values sent between devices are 32-bit elements; how exact they have to be, the bound alone decides.
No kernel may reach another device: no remote copies, remote signals or barrier semaphores. Data moves between devices by JAX's collectives and lax.ppermute only.
A program may use at most 64 MiB of HBM per device.

```python
import math
import jax
import jax.numpy as jnp
from jax import lax

TILE = 512
BAND = 64
SOURCE_GRID = 101
DOSES = 8
MAXT_DEV = 2
TILES = 64
CLIPS = 16
SRC_LIT = 32


def draw_source_index(key, part):
    key = jax.random.fold_in(key, 11)
    first_key, second_key = jax.random.split(key, 2)
    inner = 1 + jax.random.permutation(first_key, SOURCE_GRID * SOURCE_GRID - 2)[:SRC_LIT - 2]
    corners = jnp.array([0, SOURCE_GRID * SOURCE_GRID - 1], jnp.int32)
    chosen = jnp.concatenate([corners, inner.astype(jnp.int32)])
    return chosen[jax.random.permutation(second_key, SRC_LIT)]


def draw_tile_count(key, part):
    key = jax.random.fold_in(key, 12)
    first_key, second_key = jax.random.split(key, 2)
    counts = jax.random.randint(first_key, (CLIPS,), 1, 2 * MAXT_DEV + 1, dtype=jnp.int32)
    spots = jax.random.permutation(second_key, CLIPS)[:2]
    counts = counts.at[spots[0]].set(2 * MAXT_DEV)
    return counts.at[spots[1]].set(1)


def with_ends(drawn, own_key, least, largest):
    dims = drawn.shape
    spot = [jax.random.randint(jax.random.fold_in(own_key, axis), (), 0, dims[axis]) for axis in range(len(dims))]
    drawn = drawn.at[tuple(spot)].set(least)
    longest = dims.index(max(dims))
    spot[longest] = (spot[longest] + 1) % dims[longest]
    return drawn.at[tuple(spot)].set(largest)


def levels(own_key, dims, cuts, least, top_value):
    def one(dim, blocks):
        steps = jax.random.uniform(jax.random.fold_in(jax.random.fold_in(own_key, 6), dim), (blocks,), jnp.float32, least / len(cuts), top_value / len(cuts))
        return jnp.repeat(jnp.exp(steps), dims[dim] // blocks).reshape((-1,) + (1,) * (len(dims) - dim - 1))

    gain = one(*cuts[0])
    for cut in cuts[1:]:
        gain = gain * one(*cut)
    return gain


def bell_draw(stream_key, shape, deviation, bound, cuts=(), held_as=jnp.bfloat16):
    gain = levels(stream_key, shape, cuts, -0.22, 0.18) if cuts else 1.0
    values = jax.random.normal(stream_key, shape, jnp.float32) * deviation * gain
    return jnp.minimum(jnp.maximum(values, -bound), bound).astype(held_as)


def setup_inputs(seed: int = 0) -> dict:
    streams_of = jax.random.split(jax.random.key(seed), 8)
    return {
        "mask_field": bell_draw(streams_of[0], (TILES, TILE, TILE), 1.0, 6.0, ((0, 32),), jnp.float32),
        "dose_code": with_ends(jax.random.randint(streams_of[1], (TILES, DOSES, TILE, TILE), 0, 16), jax.random.fold_in(streams_of[1], 1), 0, 15).astype(jnp.int32),
        "target": jnp.clip(1.0 * jax.random.uniform(streams_of[2], (TILES, TILE, TILE), jnp.float32) ** levels(streams_of[2], (TILES, TILE, TILE), ((0, 32), (1, 16)), -0.2, 0.2), 0.0, 1.0),
        "pupil": bell_draw(streams_of[3], (2, BAND, BAND), 0.7, 4.0, (), jnp.float32),
        "source_index": draw_source_index(jax.random.fold_in(streams_of[7], 71), 0),
        "source_weight": jnp.clip(jnp.exp(math.log(0.0625) - 1.3862944 * jax.random.uniform(streams_of[5], (SRC_LIT,), jnp.float32) ** levels(streams_of[5], (SRC_LIT,), ((0, 16),), -0.2, 0.2)), 0.015625, 0.0625),
        "tile_count": draw_tile_count(jax.random.fold_in(streams_of[7], 71), 0),
    }


highest = lax.Precision.HIGHEST
steepness = 4.0
threshold = 1.0
dose_base = 0.85
dose_step = 0.02

def tables(extent, passband):
    frequency = jnp.arange(2 * passband, dtype=jnp.int32) - passband
    position = jnp.arange(extent, dtype=jnp.int32)
    angles = (frequency[:, None] * position[None, :] % extent).astype(jnp.float32) * (2.0 * math.pi / extent)
    return (jnp.cos(angles), jnp.sin(angles))

def offsets(source_index, passband):
    middle = SOURCE_GRID // 2
    grid_row = source_index // SOURCE_GRID
    grid_col = source_index % SOURCE_GRID
    row_at = (grid_row - middle) * (passband // 2) // middle + passband // 2
    col_at = (grid_col - middle) * (passband // 2) // middle + passband // 2
    return (row_at.astype(jnp.int32), col_at.astype(jnp.int32))

def mdot(left_arr, right_arr):
    return jnp.dot(left_arr, right_arr, precision=highest)

def tile_intensity(tile_mask, weights, row_at, col_at, pupil, cosine_table, sine_table):
    fwd_cos = cosine_table / math.sqrt(TILE)
    fwd_sin = sine_table / math.sqrt(TILE)
    back_cos = cosine_table.T / math.sqrt(BAND)
    back_sin = sine_table.T / math.sqrt(BAND)
    spec_real = mdot(mdot(fwd_cos, tile_mask), fwd_cos.T) - mdot(mdot(fwd_sin, tile_mask), fwd_sin.T)
    spec_imag = -(mdot(mdot(fwd_sin, tile_mask), fwd_cos.T) + mdot(mdot(fwd_cos, tile_mask), fwd_sin.T))
    zero_at = jnp.zeros((), jnp.int32)

    def add_source(running, source_item):
        weight, row_pos, col_pos = source_item
        block_re = lax.dynamic_slice(spec_real, (row_pos, col_pos), (BAND, BAND))
        block_im = lax.dynamic_slice(spec_imag, (row_pos, col_pos), (BAND, BAND))
        held_re = pupil[0] * block_re - pupil[1] * block_im
        held_im = pupil[0] * block_im + pupil[1] * block_re
        row_cos = lax.dynamic_slice(back_cos, (zero_at, row_pos), (TILE, BAND))
        row_sin = lax.dynamic_slice(back_sin, (zero_at, row_pos), (TILE, BAND))
        col_cos = lax.dynamic_slice(back_cos, (zero_at, col_pos), (TILE, BAND))
        col_sin = lax.dynamic_slice(back_sin, (zero_at, col_pos), (TILE, BAND))
        half_re = mdot(held_re, col_cos.T) - mdot(held_im, col_sin.T)
        half_im = mdot(held_re, col_sin.T) + mdot(held_im, col_cos.T)
        field_re = mdot(row_cos, half_re) - mdot(row_sin, half_im)
        field_im = mdot(row_cos, half_im) + mdot(row_sin, half_re)
        return (running + weight * (field_re * field_re + field_im * field_im), None)
    blank = jnp.zeros((TILE, TILE), jnp.float32)
    result, unused = lax.scan(add_source, blank, (weights, row_at, col_at))
    return result

def reference(mask_field, dose_code, target, pupil, source_index, source_weight, tile_count):
    cosine_table, sine_table = tables(TILE, BAND)
    row_at, col_at = offsets(source_index, BAND)
    per_clip = 2 * MAXT_DEV
    slot_ids = jnp.arange(TILES, dtype=jnp.int32)
    live = (slot_ids % per_clip < tile_count[slot_ids // per_clip]).astype(jnp.float32)

    def per_tile(tile_item):
        tile_mask, code_map, goal_map, live_flag = tile_item
        dose_value = dose_base + dose_step * code_map.astype(jnp.float32)

        def loss_of(mask_now, weights):
            intensity = tile_intensity(mask_now, weights, row_at, col_at, pupil, cosine_table, sine_table)
            printed = jax.nn.sigmoid(steepness * (dose_value * intensity[None] - threshold))
            return live_flag * jnp.sum((printed - goal_map[None]) ** 2)
        loss_value, pullback = jax.vjp(loss_of, tile_mask, source_weight)
        mask_grads, weight_grads = pullback(jnp.ones_like(loss_value))
        return (mask_grads, weight_grads)
    mask_grads, weight_grads = lax.map(per_tile, (mask_field, dose_code, target, live))
    return (mask_grads, lax.optimization_barrier(jnp.sum(weight_grads, axis=0)) / (TILE * TILE))
```

```python
import functools
import math

import jax
import jax.numpy as jnp
import numpy as np
from jax import lax
from jax.experimental import pallas as pl
from jax.experimental.pallas import tpu as pltpu
from jax.sharding import PartitionSpec as P

SOURCE_GRID = 101
TILE = 512
BAND = 64
WIDTH = 128
SRC = 16
ROWS = TILE // SRC
DOSES = 8
POINTS = 32
CHUNK = 2 * ROWS + 8

f32 = jnp.float32
bf16 = jnp.bfloat16


def halves(table):
    whole = np.asarray(table, np.float32)
    high = whole.astype(jnp.bfloat16)
    low = (whole - high.astype(np.float32)).astype(jnp.bfloat16)
    return high, low


def as_left(table):
    high, low = halves(table)
    return np.concatenate([high, high, low], -1)


def as_right(table):
    high, low = halves(table)
    return np.concatenate([high, low, high], -2)


def angles(frequency, position):
    turns = np.outer(np.asarray(frequency), np.asarray(position)) % TILE
    return turns * (2.0 * math.pi / TILE)


@functools.cache
def constants():
    pixel = np.arange(TILE)
    coarse = np.arange(WIDTH) * (TILE // WIDTH)
    wide = np.arange(WIDTH) - BAND
    narrow = np.arange(BAND)
    held = {}
    fwd = angles(wide, pixel)
    fwd_cos = np.cos(fwd) / math.sqrt(TILE)
    fwd_sin = np.sin(fwd) / math.sqrt(TILE)
    pair = np.concatenate([fwd_cos, fwd_sin], 0)
    held["spec_right"] = np.stack(halves(pair.T))
    held["spec_left"] = np.stack(halves(pair))
    row = angles(pixel, narrow)
    row_cos = np.cos(row) / math.sqrt(BAND)
    row_sin = np.sin(row) / math.sqrt(BAND)
    high, low = halves(np.concatenate([row_cos, row_sin], 1).reshape(SRC, ROWS, WIDTH))
    held["row"] = np.concatenate(
        [np.concatenate([high, high], 2), np.concatenate([low, 0 * low], 2)], 1
    )
    back = np.stack(
        [
            np.concatenate([row_cos[at : at + ROWS].T, row_sin[at : at + ROWS].T], 1)
            for at in range(0, TILE, ROWS)
        ]
    )
    held["row_back"] = as_left(back)
    col = angles(narrow, coarse)
    col_cos = np.cos(col) / math.sqrt(BAND)
    col_sin = np.sin(col) / math.sqrt(BAND)
    table = np.concatenate(
        [np.concatenate([col_cos, col_sin], 1), np.concatenate([-col_sin, col_cos], 1)], 0
    )
    held["col"] = as_right(table)
    held["col_back"] = np.concatenate(halves(table.T), 1)
    gap = pixel[None, :] - coarse[:, None]
    raised = sum(np.cos((2.0 * math.pi / TILE) * (f * gap % TILE)) for f in range(1, BAND))
    raised = (1.0 + 2.0 * raised) / WIDTH
    held["raise"] = as_right(raised)
    held["lower"] = as_right(raised.T)
    order = np.arange(1, BAND + 1)
    even = (np.abs(wide)[:, None] == order).astype(np.float32)
    odd = (wide[:, None] == order).astype(np.float32) - (wide[:, None] == -order)
    none = np.zeros_like(even)
    held["fold"] = np.concatenate(
        [
            np.concatenate([even, none, none, -odd], 1),
            np.concatenate([none, -odd, -even, none], 1),
        ],
        0,
    ).astype(jnp.bfloat16)
    final = angles(order, pixel)
    held["image"] = as_right(np.concatenate([np.cos(final), np.sin(final)], 0) / math.sqrt(TILE))
    return held


def split(value):
    high = value.astype(bf16)
    low = (value - high.astype(f32)).astype(bf16)
    return high, low


def split_cols(value):
    high, low = split(value)
    return jnp.concatenate([high, high, low], 1)


def split_rows(value):
    high, low = split(value)
    return jnp.concatenate([high, low, high], 0)


def mm(left, right):
    return jnp.dot(left, right, preferred_element_type=f32)


def pack_kernel(index_ref, weight_ref, out_ref):
    lane = lax.broadcasted_iota(jnp.int32, out_ref.shape, 2)
    packed = jnp.where(lane == 0, index_ref[0], jnp.where(lane == 1, index_ref[1], 0))
    weights = jnp.where(lane == 2, weight_ref[0], jnp.where(lane == 3, weight_ref[1], 0.0))
    out_ref[...] = packed.astype(f32) + weights


def swap_sign(value, first_half):
    turned = pltpu.roll(value, BAND, 1)
    return jnp.where(first_half, -turned, turned)


def place_of(number):
    point = number.astype(jnp.int32)
    grid_row = (point * 41529) >> 22
    grid_col = point - SOURCE_GRID * grid_row
    return ((grid_row * (16 * 5243)) >> 17, (grid_col * (16 * 5243)) >> 17)


def main_kernel(
    count_ref,
    point_ref,
    pupil_ref,
    mask_hbm,
    right_hbm,
    left_hbm,
    dose_hbm,
    target_hbm,
    raise_hbm,
    lower_hbm,
    col_back_hbm,
    fold_hbm,
    row_hbm,
    row_back_hbm,
    col_hbm,
    out_ref,
    mask_ref,
    right_ref,
    left_ref,
    dose_ref,
    target_ref,
    raise_ref,
    lower_ref,
    col_back_ref,
    fold_ref,
    row_ref,
    row_back_ref,
    col_ref,
    re_ref,
    im_ref,
    half_ref,
    field_ref,
    total_ref,
    slope_ref,
    back_ref,
    adj_ref,
    term_ref,
    sems,
):
    clip = lax.axis_index("clip")
    me = lax.axis_index("src")
    half_tile = TILE // 2
    loads = [
        pltpu.make_async_copy(source, target, sems.at[n])
        for n, (source, target) in enumerate(
            (
                (right_hbm, right_ref),
                (mask_hbm.at[0, :half_tile], mask_ref.at[0, :half_tile]),
                (mask_hbm.at[0, half_tile:], mask_ref.at[0, half_tile:]),
                (left_hbm, left_ref),
                (mask_hbm.at[1, :half_tile], mask_ref.at[1, :half_tile]),
                (mask_hbm.at[1, half_tile:], mask_ref.at[1, half_tile:]),
                (row_hbm.at[me], row_ref),
                (col_hbm, col_ref),
                (dose_hbm, dose_ref),
                (target_hbm, target_ref),
                (raise_hbm, raise_ref),
                (lower_hbm, lower_ref),
                (col_back_hbm, col_back_ref),
                (row_back_hbm.at[me], row_back_ref),
                (fold_hbm, fold_ref),
            )
        )
    ]
    for load in loads:
        load.start()
    first_half = lax.broadcasted_iota(jnp.int32, (BAND, WIDTH), 1) < BAND
    total_ref[...] = jnp.zeros_like(total_ref)
    adj_ref[...] = jnp.zeros_like(adj_ref)
    term_ref[...] = jnp.zeros_like(term_ref)
    rows = 2 * ROWS
    pupil_both = [jnp.concatenate([pupil_ref[n], pupil_ref[n]], 1) for n in range(2)]

    loads[0].wait()
    for t in range(2):
        highs = []
        lows = []
        for part in range(2):
            loads[1 + 3 * t + part].wait()
            high, low = split(mask_ref[t, part * half_tile : (part + 1) * half_tile])
            high, low = split(
                mm(high, right_ref[0]) + mm(high, right_ref[1]) + mm(low, right_ref[0])
            )
            highs.append(high)
            lows.append(low)
        high = jnp.concatenate(highs, 0)
        low = jnp.concatenate(lows, 0)
        if t == 0:
            loads[3].wait()
        blocks = mm(left_ref[0], high) + mm(left_ref[0], low) + mm(left_ref[1], high)
        re_ref[t] = blocks[:WIDTH, :WIDTH] - blocks[WIDTH:, WIDTH:]
        im_ref[t] = -(blocks[WIDTH:, :WIDTH] + blocks[:WIDTH, WIDTH:])
    loads[6].wait()
    loads[7].wait()

    def weight_of(k):
        return point_ref[k >> 1, 0, 2 + (k & 1)]

    def window_of(k):
        return place_of(point_ref[k >> 1, 0, k & 1])

    def windows(step, carry):
        for inner in range(8):
            k = step * 8 + inner
            row_pos, col_pos = window_of(k)
            back = (WIDTH - col_pos) & (WIDTH - 1)
            back_half = (WIDTH + BAND - col_pos) & (WIDTH - 1)
            held = []
            for t in range(2):
                window = jnp.where(
                    first_half,
                    pltpu.roll(re_ref[t, pl.ds(row_pos, BAND), :], back, 1),
                    pltpu.roll(im_ref[t, pl.ds(row_pos, BAND), :], back_half, 1),
                )
                turned = swap_sign(window, first_half)
                pupil_re, pupil_im = pupil_both
                high, low = split(
                    jnp.concatenate(
                        [
                            pupil_re * window + pupil_im * turned,
                            pupil_re * turned - pupil_im * window,
                        ],
                        0,
                    )
                )
                held.append(jnp.concatenate([high, low], 0))
            half = mm(row_ref[...], jnp.concatenate(held, 1))
            half = half[:ROWS] + half[ROWS:]
            half = jnp.concatenate([half[:, :WIDTH], half[:, WIDTH:]], 0)
            half_ref[pl.ds(pl.multiple_of(k * rows, rows), rows), :] = split_cols(half)
        return carry

    lax.fori_loop(0, POINTS // 8, windows, 0)

    def fields(step, carry):
        field = mm(
            half_ref[pl.ds(pl.multiple_of(step * 8 * rows, 8 * rows), 8 * rows), :], col_ref[...]
        )
        total = total_ref[...]
        for inner in range(8):
            k = step * 8 + inner
            one = field[inner * rows : (inner + 1) * rows]
            field_ref[k] = one
            total += weight_of(k) * (
                one[:, :WIDTH] * one[:, :WIDTH] + one[:, WIDTH:] * one[:, WIDTH:]
            )
        total_ref[...] = total
        return carry

    lax.fori_loop(0, POINTS // 8, fields, 0)

    for load in loads[8:]:
        load.wait()
    intensity = mm(split_cols(total_ref[...]), raise_ref[...])
    for t in range(2):
        slot = (clip & 1) * 2 + t
        live = jnp.where(slot < count_ref[clip >> 1], 1.0, 0.0).astype(f32)
        bright = intensity[t * ROWS : (t + 1) * ROWS]
        goal = target_ref[t]
        slope = jnp.zeros((ROWS, TILE), f32)
        for s in range(DOSES):
            dose = 0.85 + 0.02 * dose_ref[t, s].astype(f32)
            printed = 1.0 / (1.0 + jnp.exp(-4.0 * (dose * bright - 1.0)))
            slope += (printed - goal) * (printed * (1.0 - printed)) * dose
        slope_ref[t * ROWS : (t + 1) * ROWS] = (8.0 * live) * slope
    slope_ref[:, :WIDTH] = mm(split_cols(slope_ref[...]), lower_ref[...])

    def columns_back(step, carry):
        slope = slope_ref[:, :WIDTH]
        highs = []
        lows = []
        for inner in range(8):
            k = step * 8 + inner
            field = field_ref[k]
            weighed_re = slope * field[:, :WIDTH]
            weighed_im = slope * field[:, WIDTH:]
            term = jnp.sum(
                weighed_re * field[:, :WIDTH] + weighed_im * field[:, WIDTH:], 0, keepdims=True
            )
            term_ref[step * 4 + inner // 2, 2 + inner % 2 : 3 + inner % 2, :] = term
            twice = 2.0 * weight_of(k)
            high, low = split(jnp.concatenate([twice * weighed_re, twice * weighed_im], 1))
            highs.append(high)
            lows.append(low)
        half = mm(jnp.concatenate(highs, 0), col_back_ref[...])
        rest = mm(jnp.concatenate(lows, 0), col_back_ref[:, :WIDTH])
        back_ref[pl.ds(pl.multiple_of(step * 8 * rows, 8 * rows), 8 * rows), :] = (
            half[:, :WIDTH] + half[:, WIDTH:] + rest
        )
        return carry

    lax.fori_loop(0, POINTS // 8, columns_back, 0)

    def rows_back(step, carry):
        for inner in range(8):
            k = step * 8 + inner
            row_pos, col_pos = window_of(k)
            half = back_ref[pl.ds(pl.multiple_of(k * rows, rows), rows), :]
            turned = -swap_sign(half, first_half)
            pair = jnp.concatenate(
                [
                    split_rows(jnp.concatenate([half[:ROWS], turned[:ROWS]], 0)),
                    split_rows(jnp.concatenate([half[ROWS:], turned[ROWS:]], 0)),
                ],
                1,
            )
            both = mm(row_back_ref[...], pair)
            for t in range(2):
                held = both[:, t * WIDTH : (t + 1) * WIDTH]
                spread = pupil_both[0] * held - pupil_both[1] * swap_sign(held, first_half)
                spread_re = pltpu.roll(jnp.where(first_half, spread, 0.0), col_pos, 1)
                spread_im = pltpu.roll(jnp.where(first_half, 0.0, spread), col_pos + BAND, 1)
                adj_ref[t, pl.ds(row_pos, BAND), :] += spread_re
                adj_ref[2 + t, pl.ds(row_pos, BAND), :] += spread_im
        return carry

    lax.fori_loop(0, POINTS // 8, rows_back, 0)

    lane = lax.broadcasted_iota(jnp.int32, (WIDTH, WIDTH), 1)
    tops = []
    bottoms = []
    top_flat = jnp.zeros((WIDTH, WIDTH), f32)
    bottom_flat = jnp.zeros((WIDTH, WIDTH), f32)
    for t in range(2):
        adj_re = adj_ref[t]
        adj_im = adj_ref[2 + t]
        high, low = split(jnp.concatenate([adj_re, adj_im], 1))
        folded = mm(high, fold_ref[...]) + mm(low, fold_ref[...])
        tops.append(folded[:, :WIDTH])
        bottoms.append(folded[:, WIDTH:])
        top_flat += jnp.where(lane == t, pltpu.roll(adj_re, BAND + t, 1), 0.0)
        bottom_flat -= jnp.where(lane == t, pltpu.roll(adj_im, BAND + t, 1), 0.0)
    high, low = split(
        jnp.concatenate(
            [
                jnp.concatenate(tops + [top_flat], 1),
                jnp.concatenate(bottoms + [bottom_flat], 1),
            ],
            0,
        )
    )
    for block in range(4):
        at_rows = slice(block * WIDTH, (block + 1) * WIDTH)
        table_high = right_ref[0, at_rows, :]
        lines = mm(table_high, high) + mm(table_high, low) + mm(right_ref[1, at_rows, :], high)
        flat = lines[:, 2 * WIDTH :].T
        for n in range(4):
            owner = block * 4 + n
            own_rows = lines[n * ROWS : (n + 1) * ROWS]
            out_ref[owner, :ROWS, :] = own_rows[:, :WIDTH]
            out_ref[owner, ROWS:rows, :] = own_rows[:, WIDTH : 2 * WIDTH]
            out_ref[owner, rows:, :] = flat[:8] + term_ref[owner]


def image_kernel(chunk_ref, table_ref, out_ref, term_ref):
    me = lax.axis_index("src")
    rows = 2 * ROWS
    total = jnp.sum(chunk_ref[...], 0)
    image = mm(split_cols(total[:rows]), table_ref[...])
    last = total[rows:]
    flat = pltpu.roll(last, (WIDTH - (me & 3) * ROWS) & (WIDTH - 1), 1)
    diagonal = lax.broadcasted_iota(jnp.int32, (ROWS, WIDTH), 0) == lax.broadcasted_iota(
        jnp.int32, (ROWS, WIDTH), 1
    )
    for t in range(2):
        column = jnp.sum(jnp.where(diagonal, flat[t : t + 1], 0.0), 1, keepdims=True)
        out_ref[t] = image[t * ROWS : (t + 1) * ROWS] + column * (1.0 / math.sqrt(TILE))
    sums = jnp.sum(last, 1, keepdims=True) * (1.0 / (TILE * TILE))
    term_ref[...] = jnp.broadcast_to(jnp.broadcast_to(sums, (8, WIDTH))[None], term_ref.shape)


def whole(array):
    return pl.BlockSpec(array.shape, lambda *_: (0,) * array.ndim)


def clip_groups(clips, bits):
    rest = [c for c in range(clips) if not c & bits]
    return [[base | c for c in range(clips) if not c & ~bits] for base in rest]


def per_device(
    clips, mask_field, dose_code, target, pupil, source_index, source_weight, tile_count
):
    held = {name: jnp.asarray(table) for name, table in constants().items()}
    smem = pl.BlockSpec(memory_space=pltpu.SMEM)
    hbm = pl.BlockSpec(memory_space=pltpu.HBM)

    mine = pl.pallas_call(
        pack_kernel,
        in_specs=[smem, smem],
        out_shape=jax.ShapeDtypeStruct((SRC, 8, WIDTH), f32),
        name="pack",
    )(source_index, source_weight)
    points = lax.all_to_all(mine, "src", 0, 0)

    tables = [
        held[n]
        for n in (
            "spec_right",
            "spec_left",
            "raise",
            "lower",
            "col_back",
            "fold",
            "row",
            "row_back",
            "col",
        )
    ]
    stored = [mask_field, *tables[:2], dose_code, target, *tables[2:]]
    landing = [
        pltpu.VMEM(a.shape[1:] if n in (9, 10) else a.shape, a.dtype)
        for n, a in enumerate(stored)
    ]
    blocks = pl.pallas_call(
        main_kernel,
        in_specs=[smem, smem, whole(pupil)] + [hbm] * len(stored),
        out_shape=jax.ShapeDtypeStruct((SRC, CHUNK, WIDTH), f32),
        scratch_shapes=landing
        + [
            pltpu.VMEM((2, WIDTH, WIDTH), f32),
            pltpu.VMEM((2, WIDTH, WIDTH), f32),
            pltpu.VMEM((POINTS * 2 * ROWS, 3 * WIDTH), bf16),
            pltpu.VMEM((POINTS, 2 * ROWS, 2 * WIDTH), f32),
            pltpu.VMEM((2 * ROWS, WIDTH), f32),
            pltpu.VMEM((2 * ROWS, TILE), f32),
            pltpu.VMEM((POINTS * 2 * ROWS, WIDTH), f32),
            pltpu.VMEM((4, WIDTH, WIDTH), f32),
            pltpu.VMEM((SRC, 8, WIDTH), f32),
            pltpu.SemaphoreType.DMA((len(stored) + 3,)),
        ],
        compiler_params=pltpu.CompilerParams(vmem_limit_bytes=30 * 1024 * 1024),
        cost_estimate=pl.CostEstimate(
            flops=3_000_000_000, bytes_accessed=5_000_000, transcendentals=300_000
        ),
        name="fields",
    )(tile_count, points, pupil, *stored)

    chunks = lax.all_to_all(blocks, "src", 0, 0)
    near = 4 if clips == 32 else 1
    grad_mask, term = pl.pallas_call(
        image_kernel,
        out_shape=[
            jax.ShapeDtypeStruct((2, ROWS, TILE), f32),
            jax.ShapeDtypeStruct((near, 8, WIDTH), f32),
        ],
        compiler_params=pltpu.CompilerParams(vmem_limit_bytes=12 * 1024 * 1024),
        cost_estimate=pl.CostEstimate(
            flops=100_000_000, bytes_accessed=1_000_000, transcendentals=0
        ),
        name="image",
    )(chunks, held["image"])
    if clips == 32:
        term = lax.all_to_all(term, "clip", 0, 0, axis_index_groups=clip_groups(clips, 17))
        term = jnp.broadcast_to(jnp.sum(term, 0), (8, 8, WIDTH))
        term = lax.all_to_all(term, "clip", 0, 0, axis_index_groups=clip_groups(clips, 14))
    grad_source = jnp.sum(term[:, 2:4, 0], 0)
    return (grad_mask, grad_source)


def solution(mesh):
    return jax.shard_map(
        functools.partial(per_device, mesh.shape["clip"]),
        mesh=mesh,
        in_specs=(
            P("clip", None, None),
            P("clip", None, "src", None),
            P("clip", "src", None),
            P(),
            P("src"),
            P("src"),
            P(),
        ),
        out_specs=(P("clip", "src", None), P("src")),
        check_vma=False,
    )
```

```python
import functools
import math

import jax
import jax.numpy as jnp
import numpy as np
from jax import lax
from jax.experimental import pallas as pl
from jax.experimental.pallas import tpu as pltpu
from jax.sharding import PartitionSpec as P

SOURCE_GRID = 101
TILE = 512
BAND = 64
WIDTH = 128
SRC = 16
ROWS = TILE // SRC
DOSES = 8
POINTS = 32
CHUNK = 2 * ROWS + 8

f32 = jnp.float32
bf16 = jnp.bfloat16


def halves(table):
    whole = np.asarray(table, np.float32)
    high = whole.astype(jnp.bfloat16)
    low = (whole - high.astype(np.float32)).astype(jnp.bfloat16)
    return high, low


def as_left(table):
    high, low = halves(table)
    return np.concatenate([high, high, low], -1)


def as_right(table):
    high, low = halves(table)
    return np.concatenate([high, low, high], -2)


def angles(frequency, position):
    turns = np.outer(np.asarray(frequency), np.asarray(position)) % TILE
    return turns * (2.0 * math.pi / TILE)


@functools.cache
def constants():
    pixel = np.arange(TILE)
    coarse = np.arange(WIDTH) * (TILE // WIDTH)
    wide = np.arange(WIDTH) - BAND
    narrow = np.arange(BAND)
    held = {}
    fwd = angles(wide, pixel)
    fwd_cos = np.cos(fwd) / math.sqrt(TILE)
    fwd_sin = np.sin(fwd) / math.sqrt(TILE)
    pair = np.concatenate([fwd_cos, fwd_sin], 0)
    held["spec_right"] = np.stack(halves(pair.T))
    held["spec_left"] = np.stack(halves(pair))
    row = angles(pixel, narrow)
    row_cos = np.cos(row) / math.sqrt(BAND)
    row_sin = np.sin(row) / math.sqrt(BAND)
    lines = []
    backs = []
    for at in range(0, TILE, ROWS):
        high, low = halves(
            np.concatenate([row_cos[at : at + ROWS], row_sin[at : at + ROWS]], 0)
        )
        lines.append(
            np.concatenate(
                [np.concatenate([high, high], 1), np.concatenate([low, 0 * low], 1)], 0
            )
        )
        backs.append(
            as_left(np.concatenate([row_cos[at : at + ROWS].T, row_sin[at : at + ROWS].T], 0))
        )
    held["row"] = np.stack(lines)
    held["row_back"] = np.stack(backs)
    col = angles(narrow, coarse)
    col_cos = np.cos(col) / math.sqrt(BAND)
    col_sin = np.sin(col) / math.sqrt(BAND)
    table = np.concatenate(
        [np.concatenate([col_cos, col_sin], 1), np.concatenate([-col_sin, col_cos], 1)], 0
    )
    held["col"] = as_right(table)
    held["col_back"] = np.concatenate(halves(table.T), 1)
    gap = pixel[None, :] - coarse[:, None]
    raised = sum(np.cos((2.0 * math.pi / TILE) * (f * gap % TILE)) for f in range(1, BAND))
    raised = (1.0 + 2.0 * raised) / WIDTH
    held["raise"] = as_right(raised)
    held["lower"] = as_right(raised.T)
    order = np.arange(1, BAND + 1)
    even = (np.abs(wide)[:, None] == order).astype(np.float32)
    odd = (wide[:, None] == order).astype(np.float32) - (wide[:, None] == -order)
    none = np.zeros_like(even)
    held["fold"] = np.concatenate(
        [
            np.concatenate([even, none, none, -odd], 1),
            np.concatenate([none, -odd, -even, none], 1),
        ],
        0,
    ).astype(jnp.bfloat16)
    final = angles(order, pixel)
    held["image"] = as_right(np.concatenate([np.cos(final), np.sin(final)], 0) / math.sqrt(TILE))
    return held


def split(value):
    high = value.astype(bf16)
    low = (value - high.astype(f32)).astype(bf16)
    return high, low


def split_cols(value):
    high, low = split(value)
    return jnp.concatenate([high, high, low], 1)


def split_rows(value):
    high, low = split(value)
    return jnp.concatenate([high, low, high], 0)


def mm(left, right):
    return jnp.dot(left, right, preferred_element_type=f32)


def pack_kernel(index_ref, weight_ref, out_ref):
    lane = lax.broadcasted_iota(jnp.int32, out_ref.shape, 2)
    packed = jnp.where(lane == 0, index_ref[0], jnp.where(lane == 1, index_ref[1], 0))
    weights = jnp.where(lane == 2, weight_ref[0], jnp.where(lane == 3, weight_ref[1], 0.0))
    out_ref[...] = packed.astype(f32) + weights


def spectrum_kernel(
    mask_hbm, right_hbm, left_hbm, after_hbm, re_ref, im_ref, mask_ref, right_ref, left_ref, sems
):
    half_tile = TILE // 2
    pairs = [(right_hbm, right_ref)]
    for t in range(2):
        for part in range(2):
            rows = pl.ds(part * half_tile, half_tile)
            pairs.append((mask_hbm.at[t, rows], mask_ref.at[t, rows]))
    pairs.insert(3, (left_hbm, left_ref))
    loads = [pltpu.make_async_copy(*pair, sems.at[n]) for n, pair in enumerate(pairs)]
    for load in loads:
        load.start()
    loads[0].wait()
    for t in range(2):
        highs = []
        lows = []
        for part in range(2):
            loads[1 + 3 * t + part].wait()
            high, low = split(mask_ref[t, part * half_tile : (part + 1) * half_tile])
            high, low = split(
                mm(high, right_ref[0]) + mm(high, right_ref[1]) + mm(low, right_ref[0])
            )
            highs.append(high)
            lows.append(low)
        high = jnp.concatenate(highs, 0)
        low = jnp.concatenate(lows, 0)
        if t == 0:
            loads[3].wait()
        blocks = mm(left_ref[0], high) + mm(left_ref[0], low) + mm(left_ref[1], high)
        re_ref[t] = blocks[:WIDTH, :WIDTH] - blocks[WIDTH:, WIDTH:]
        im_ref[t] = pltpu.roll(-(blocks[WIDTH:, :WIDTH] + blocks[:WIDTH, WIDTH:]), BAND, 1)


def place_of(number):
    point = number.astype(jnp.int32)
    grid_row = (point * 41529) >> 22
    grid_col = point - SOURCE_GRID * grid_row
    return ((grid_row * (16 * 5243)) >> 17, (grid_col * (16 * 5243)) >> 17)


def main_kernel(
    point_hbm,
    count_hbm,
    re_hbm,
    im_hbm,
    pupil_hbm,
    row_hbm,
    col_hbm,
    dose_hbm,
    target_hbm,
    raise_hbm,
    lower_hbm,
    col_back_hbm,
    row_back_hbm,
    fold_hbm,
    lines_hbm,
    out_ref,
    point_ref,
    count_ref,
    re_ref,
    im_ref,
    pupil_ref,
    row_ref,
    col_ref,
    dose_ref,
    target_ref,
    raise_ref,
    lower_ref,
    col_back_ref,
    row_back_ref,
    fold_ref,
    right_ref,
    half_ref,
    field_ref,
    total_ref,
    slope_ref,
    back_ref,
    adj_ref,
    term_ref,
    sems,
):
    clip = lax.axis_index("clip")
    me = lax.axis_index("src")
    loads = [
        pltpu.make_async_copy(source, target, sems.at[n])
        for n, (source, target) in enumerate(
            (
                (point_hbm, point_ref),
                (re_hbm, re_ref),
                (im_hbm, im_ref),
                (pupil_hbm, pupil_ref),
                (row_hbm.at[me], row_ref),
                (col_hbm, col_ref),
                (dose_hbm, dose_ref),
                (raise_hbm, raise_ref),
                (target_hbm, target_ref),
                (count_hbm, count_ref),
                (lower_hbm, lower_ref),
                (col_back_hbm, col_back_ref),
                (row_back_hbm.at[me], row_back_ref),
                (fold_hbm, fold_ref),
                (lines_hbm, right_ref),
            )
        )
    ]
    for load in loads:
        load.start()
    lane = lax.broadcasted_iota(jnp.int32, (BAND, WIDTH), 1)
    first_half = lane < BAND
    total_ref[...] = jnp.zeros_like(total_ref)
    adj_ref[...] = jnp.zeros_like(adj_ref)
    term_ref[...] = jnp.zeros_like(term_ref)
    rows = 2 * ROWS
    for load in loads[:5]:
        load.wait()
    pupil_re, pupil_im = [jnp.concatenate([pupil_ref[n], pupil_ref[n]], 1) for n in range(2)]
    pupil_re_odd = jnp.where(first_half, -pupil_re, pupil_re)
    pupil_im_odd = jnp.where(first_half, -pupil_im, pupil_im)
    odd = jnp.where(first_half[:ROWS], -1.0, 1.0).astype(f32)

    def weight_of(k):
        return point_ref[k >> 1, 0, 2 + (k & 1)]

    def window_of(k):
        return place_of(point_ref[k >> 1, 0, k & 1])

    def windows(step, carry):
        for inner in range(8):
            k = step * 8 + inner
            row_pos, col_pos = window_of(k)
            inside = (lane >= col_pos) & (lane < col_pos + BAND)
            highs = []
            lows = []
            for t in range(2):
                mixed = jnp.where(
                    inside, re_ref[t, pl.ds(row_pos, BAND), :], im_ref[t, pl.ds(row_pos, BAND), :]
                )
                window = pltpu.roll(mixed, (WIDTH - col_pos) & (WIDTH - 1), 1)
                turned = pltpu.roll(mixed, (WIDTH + BAND - col_pos) & (WIDTH - 1), 1)
                high, low = split(pupil_re * window + pupil_im_odd * turned)
                highs.append(high)
                lows.append(low)
            both = mm(
                row_ref[...],
                jnp.concatenate([jnp.concatenate(highs, 1), jnp.concatenate(lows, 1)], 0),
            )
            both = both[:rows] + both[rows:]
            half = jnp.concatenate(
                [
                    both[:ROWS, at : at + WIDTH] + odd * pltpu.roll(both[ROWS:, at : at + WIDTH], BAND, 1)
                    for at in (0, WIDTH)
                ],
                0,
            )
            half_ref[pl.ds(pl.multiple_of(k * rows, rows), rows), :] = split_cols(half)
        return carry

    lax.fori_loop(0, POINTS // 8, windows, 0)
    loads[5].wait()

    def fields(step, carry):
        field = mm(
            half_ref[pl.ds(pl.multiple_of(step * 8 * rows, 8 * rows), 8 * rows), :], col_ref[...]
        )
        total = total_ref[...]
        for inner in range(8):
            k = step * 8 + inner
            one = field[inner * rows : (inner + 1) * rows]
            field_ref[k] = one
            total += weight_of(k) * (
                one[:, :WIDTH] * one[:, :WIDTH] + one[:, WIDTH:] * one[:, WIDTH:]
            )
        total_ref[...] = total
        return carry

    lax.fori_loop(0, POINTS // 8, fields, 0)

    for load in loads[6:]:
        load.wait()
    intensity = mm(split_cols(total_ref[...]), raise_ref[...])
    for t in range(2):
        slot = (clip & 1) * 2 + t
        live = jnp.where(slot < count_ref[clip >> 1], 1.0, 0.0).astype(f32)
        bright = intensity[t * ROWS : (t + 1) * ROWS]
        goal = target_ref[t]
        slope = jnp.zeros((ROWS, TILE), f32)
        for s in range(DOSES):
            dose = 0.85 + 0.02 * dose_ref[t, s].astype(f32)
            printed = 1.0 / (1.0 + jnp.exp(-4.0 * (dose * bright - 1.0)))
            slope += (printed - goal) * (printed * (1.0 - printed)) * dose
        slope_ref[t * ROWS : (t + 1) * ROWS] = (8.0 * live) * slope
    slope_ref[:, :WIDTH] = mm(split_cols(slope_ref[...]), lower_ref[...])

    def columns_back(step, carry):
        slope = slope_ref[:, :WIDTH]
        highs = []
        lows = []
        for inner in range(8):
            k = step * 8 + inner
            field = field_ref[k]
            weighed_re = slope * field[:, :WIDTH]
            weighed_im = slope * field[:, WIDTH:]
            term = jnp.sum(
                weighed_re * field[:, :WIDTH] + weighed_im * field[:, WIDTH:], 0, keepdims=True
            )
            term_ref[step * 4 + inner // 2, 2 + inner % 2 : 3 + inner % 2, :] = term
            twice = 2.0 * weight_of(k)
            high, low = split(jnp.concatenate([twice * weighed_re, twice * weighed_im], 1))
            highs.append(high)
            lows.append(low)
        half = mm(jnp.concatenate(highs, 0), col_back_ref[...])
        rest = mm(jnp.concatenate(lows, 0), col_back_ref[:, :WIDTH])
        back_ref[pl.ds(pl.multiple_of(step * 8 * rows, 8 * rows), 8 * rows), :] = (
            half[:, :WIDTH] + half[:, WIDTH:] + rest
        )
        return carry

    lax.fori_loop(0, POINTS // 8, columns_back, 0)

    def rows_back(step, carry):
        for inner in range(8):
            k = step * 8 + inner
            row_pos, col_pos = window_of(k)
            inside = (lane >= col_pos) & (lane < col_pos + BAND)
            half = back_ref[pl.ds(pl.multiple_of(k * rows, rows), rows), :]
            both = mm(
                row_back_ref[...],
                split_rows(jnp.concatenate([half[:ROWS], half[ROWS:]], 1)),
            )
            for t in range(2):
                by_cos = both[:BAND, t * WIDTH : (t + 1) * WIDTH]
                by_sin = both[BAND:, t * WIDTH : (t + 1) * WIDTH]
                straight = pupil_re * by_cos - pupil_im * by_sin
                crossed = pupil_im_odd * by_cos + pupil_re_odd * by_sin
                spread = pltpu.roll(straight, col_pos, 1) + pltpu.roll(
                    crossed, (col_pos + BAND) & (WIDTH - 1), 1
                )
                adj_ref[t, pl.ds(row_pos, BAND), :] += jnp.where(inside, spread, 0.0)
                adj_ref[2 + t, pl.ds(row_pos, BAND), :] += jnp.where(inside, 0.0, spread)
        return carry

    lax.fori_loop(0, POINTS // 8, rows_back, 0)

    lane = lax.broadcasted_iota(jnp.int32, (WIDTH, WIDTH), 1)
    tops = []
    bottoms = []
    top_flat = jnp.zeros((WIDTH, WIDTH), f32)
    bottom_flat = jnp.zeros((WIDTH, WIDTH), f32)
    for t in range(2):
        adj_re = adj_ref[t]
        adj_im = pltpu.roll(adj_ref[2 + t], BAND, 1)
        high, low = split(jnp.concatenate([adj_re, adj_im], 1))
        folded = mm(high, fold_ref[...]) + mm(low, fold_ref[...])
        tops.append(folded[:, :WIDTH])
        bottoms.append(folded[:, WIDTH:])
        top_flat += jnp.where(lane == t, pltpu.roll(adj_re, BAND + t, 1), 0.0)
        bottom_flat -= jnp.where(lane == t, pltpu.roll(adj_im, BAND + t, 1), 0.0)
    high, low = split(
        jnp.concatenate(
            [
                jnp.concatenate(tops + [top_flat], 1),
                jnp.concatenate(bottoms + [bottom_flat], 1),
            ],
            0,
        )
    )
    for block in range(4):
        at_rows = slice(block * WIDTH, (block + 1) * WIDTH)
        table_high = right_ref[0, at_rows, :]
        lines = mm(table_high, high) + mm(table_high, low) + mm(right_ref[1, at_rows, :], high)
        flat = lines[:, 2 * WIDTH :].T
        for n in range(4):
            owner = block * 4 + n
            own_rows = lines[n * ROWS : (n + 1) * ROWS]
            out_ref[owner, :ROWS, :] = own_rows[:, :WIDTH]
            out_ref[owner, ROWS:rows, :] = own_rows[:, WIDTH : 2 * WIDTH]
            out_ref[owner, rows:, :] = flat[:8] + term_ref[owner]


def image_kernel(chunk_ref, table_ref, out_ref, term_ref):
    me = lax.axis_index("src")
    rows = 2 * ROWS
    total = jnp.sum(chunk_ref[...], 0)
    image = mm(split_cols(total[:rows]), table_ref[...])
    last = total[rows:]
    flat = pltpu.roll(last, (WIDTH - (me & 3) * ROWS) & (WIDTH - 1), 1)
    diagonal = lax.broadcasted_iota(jnp.int32, (ROWS, WIDTH), 0) == lax.broadcasted_iota(
        jnp.int32, (ROWS, WIDTH), 1
    )
    for t in range(2):
        column = jnp.sum(jnp.where(diagonal, flat[t : t + 1], 0.0), 1, keepdims=True)
        out_ref[t] = image[t * ROWS : (t + 1) * ROWS] + column * (1.0 / math.sqrt(TILE))
    sums = jnp.sum(last, 1, keepdims=True) * (1.0 / (TILE * TILE))
    term_ref[...] = jnp.broadcast_to(jnp.broadcast_to(sums, (8, WIDTH))[None], term_ref.shape)


def per_device(
    clips, mask_field, dose_code, target, pupil, source_index, source_weight, tile_count
):
    held = {name: jnp.asarray(table) for name, table in constants().items()}
    smem = pl.BlockSpec(memory_space=pltpu.SMEM)
    hbm = pl.BlockSpec(memory_space=pltpu.HBM)

    mine = pl.pallas_call(
        pack_kernel,
        in_specs=[smem, smem],
        out_shape=jax.ShapeDtypeStruct((SRC, 1, WIDTH), f32),
        name="pack",
    )(source_index, source_weight)
    points = lax.all_to_all(mine, "src", 0, 0)

    roomy = pltpu.CompilerParams(vmem_limit_bytes=56 * 1024 * 1024)
    stored = [mask_field, held["spec_right"], held["spec_left"]]
    spec_shape = jax.ShapeDtypeStruct((2, WIDTH, WIDTH), f32)
    spec_re, spec_im = pl.pallas_call(
        spectrum_kernel,
        in_specs=[hbm] * 4,
        out_shape=[spec_shape, spec_shape],
        scratch_shapes=[pltpu.VMEM(a.shape, a.dtype) for a in stored]
        + [pltpu.SemaphoreType.DMA((6,))],
        compiler_params=roomy,
        cost_estimate=pl.CostEstimate(
            flops=1_200_000_000, bytes_accessed=3_000_000, transcendentals=0
        ),
        name="spectrum",
    )(*stored, mine)

    stored = [points, tile_count, spec_re, spec_im, pupil, held["row"], held["col"]]
    stored += [dose_code, target, held["raise"], held["lower"], held["col_back"]]
    stored += [held["row_back"], held["fold"], held["spec_right"]]
    landing = [pltpu.VMEM(a.shape, a.dtype) for a in stored]
    landing[0] = pltpu.SMEM(points.shape, f32)
    landing[1] = pltpu.SMEM(tile_count.shape, jnp.int32)
    for n in (5, 12):
        landing[n] = pltpu.VMEM(stored[n].shape[1:], bf16)
    blocks = pl.pallas_call(
        main_kernel,
        in_specs=[hbm] * len(stored),
        out_specs=pl.BlockSpec(memory_space=pltpu.VMEM),
        out_shape=jax.ShapeDtypeStruct((SRC, CHUNK, WIDTH), f32),
        scratch_shapes=landing
        + [
            pltpu.VMEM((POINTS * 2 * ROWS, 3 * WIDTH), bf16),
            pltpu.VMEM((POINTS, 2 * ROWS, 2 * WIDTH), f32),
            pltpu.VMEM((2 * ROWS, WIDTH), f32),
            pltpu.VMEM((2 * ROWS, TILE), f32),
            pltpu.VMEM((POINTS * 2 * ROWS, WIDTH), f32),
            pltpu.VMEM((4, WIDTH, WIDTH), f32),
            pltpu.VMEM((SRC, 8, WIDTH), f32),
            pltpu.SemaphoreType.DMA((len(stored),)),
        ],
        compiler_params=roomy,
        cost_estimate=pl.CostEstimate(
            flops=3_000_000_000, bytes_accessed=5_000_000, transcendentals=300_000
        ),
        name="fields",
    )(*stored)

    chunks = lax.all_to_all(blocks, "src", 0, 0)
    grad_mask, term = pl.pallas_call(
        image_kernel,
        out_shape=[
            jax.ShapeDtypeStruct((2, ROWS, TILE), f32),
            jax.ShapeDtypeStruct((clips, 8, WIDTH), f32),
        ],
        compiler_params=pltpu.CompilerParams(vmem_limit_bytes=12 * 1024 * 1024),
        cost_estimate=pl.CostEstimate(
            flops=100_000_000, bytes_accessed=1_000_000, transcendentals=0
        ),
        name="image",
    )(chunks, held["image"])
    term = lax.all_to_all(term, "clip", 0, 0)
    grad_source = jnp.sum(term[:, 2:4, 0], 0)
    return (grad_mask, grad_source)


def solution(mesh):
    return jax.shard_map(
        functools.partial(per_device, mesh.shape["clip"]),
        mesh=mesh,
        in_specs=(
            P("clip", None, None),
            P("clip", None, "src", None),
            P("clip", "src", None),
            P(),
            P("src"),
            P("src"),
            P(),
        ),
        out_specs=(P("clip", "src", None), P("src")),
        check_vma=False,
    )
```

```python
import functools
import math

import jax
import jax.numpy as jnp
import numpy as np
from jax import lax
from jax.experimental import pallas as pl
from jax.experimental.pallas import tpu as pltpu
from jax.sharding import PartitionSpec as P

SOURCE_GRID = 101
TILE = 512
BAND = 64
WIDTH = 128
SRC = 16
ROWS = TILE // SRC
DOSES = 8
POINTS = 32
CHUNK = 2 * ROWS + 8

f32 = jnp.float32
bf16 = jnp.bfloat16


def halves(table):
    whole = np.asarray(table, np.float32)
    high = whole.astype(jnp.bfloat16)
    low = (whole - high.astype(np.float32)).astype(jnp.bfloat16)
    return high, low


def as_left(table):
    high, low = halves(table)
    return np.concatenate([high, high, low], -1)


def as_right(table):
    high, low = halves(table)
    return np.concatenate([high, low, high], -2)


def angles(frequency, position):
    turns = np.outer(np.asarray(frequency), np.asarray(position)) % TILE
    return turns * (2.0 * math.pi / TILE)


@functools.cache
def constants():
    pixel = np.arange(TILE)
    coarse = np.arange(WIDTH) * (TILE // WIDTH)
    wide = np.arange(WIDTH) - BAND
    narrow = np.arange(BAND)
    held = {}
    fwd = angles(wide, pixel)
    fwd_cos = np.cos(fwd) / math.sqrt(TILE)
    fwd_sin = np.sin(fwd) / math.sqrt(TILE)
    pair = np.concatenate([fwd_cos, fwd_sin], 0)
    held["spec_right"] = np.stack(halves(pair.T))
    held["spec_left"] = np.stack(halves(pair))
    row = angles(pixel, narrow)
    row_cos = np.cos(row) / math.sqrt(BAND)
    row_sin = np.sin(row) / math.sqrt(BAND)
    lines = []
    backs = []
    for at in range(0, TILE, ROWS):
        high, low = halves(
            np.concatenate([row_cos[at : at + ROWS], row_sin[at : at + ROWS]], 0)
        )
        lines.append(
            np.concatenate(
                [np.concatenate([high, high], 1), np.concatenate([low, 0 * low], 1)], 0
            )
        )
        backs.append(
            as_left(np.concatenate([row_cos[at : at + ROWS].T, row_sin[at : at + ROWS].T], 0))
        )
    held["row"] = np.stack(lines)
    held["row_back"] = np.stack(backs)
    col = angles(narrow, coarse)
    col_cos = np.cos(col) / math.sqrt(BAND)
    col_sin = np.sin(col) / math.sqrt(BAND)
    table = np.concatenate(
        [np.concatenate([col_cos, col_sin], 1), np.concatenate([-col_sin, col_cos], 1)], 0
    )
    held["col"] = as_right(table)
    held["col_back"] = np.concatenate(halves(table.T), 1)
    gap = pixel[None, :] - coarse[:, None]
    raised = sum(np.cos((2.0 * math.pi / TILE) * (f * gap % TILE)) for f in range(1, BAND))
    raised = (1.0 + 2.0 * raised) / WIDTH
    held["raise"] = as_right(raised)
    held["lower"] = as_right(raised.T)
    order = np.arange(1, BAND + 1)
    even = (np.abs(wide)[:, None] == order).astype(np.float32)
    odd = (wide[:, None] == order).astype(np.float32) - (wide[:, None] == -order)
    none = np.zeros_like(even)
    held["fold"] = np.concatenate(
        [
            np.concatenate([even, none, none, -odd], 1),
            np.concatenate([none, -odd, -even, none], 1),
        ],
        0,
    ).astype(jnp.bfloat16)
    final = angles(order, pixel)
    held["image"] = as_right(np.concatenate([np.cos(final), np.sin(final)], 0) / math.sqrt(TILE))
    return held


def split(value):
    high = value.astype(bf16)
    low = (value - high.astype(f32)).astype(bf16)
    return high, low


def split_cols(value):
    high, low = split(value)
    return jnp.concatenate([high, high, low], 1)


def split_rows(value):
    high, low = split(value)
    return jnp.concatenate([high, low, high], 0)


def mm(left, right):
    return jnp.dot(left, right, preferred_element_type=f32)


def pack_kernel(index_any, weight_any, out_ref, index_ref, weight_ref, sems):
    loads = [
        pltpu.make_async_copy(index_any, index_ref, sems.at[0]),
        pltpu.make_async_copy(weight_any, weight_ref, sems.at[1]),
    ]
    for load in loads:
        load.start()
    lane = lax.broadcasted_iota(jnp.int32, out_ref.shape, 2)
    for load in loads:
        load.wait()
    packed = jnp.where(lane == 0, index_ref[0], jnp.where(lane == 1, index_ref[1], 0))
    weights = jnp.where(lane == 2, weight_ref[0], jnp.where(lane == 3, weight_ref[1], 0.0))
    out_ref[...] = packed.astype(f32) + weights


def spectrum_kernel(mask_ref, right_ref, left_ref, after_hbm, re_ref, im_ref):
    for t in range(2):
        high, low = split(mask_ref[t])
        high, low = split(mm(high, right_ref[0]) + mm(high, right_ref[1]) + mm(low, right_ref[0]))
        blocks = mm(left_ref[0], high) + mm(left_ref[0], low) + mm(left_ref[1], high)
        re_ref[t] = blocks[:WIDTH, :WIDTH] - blocks[WIDTH:, WIDTH:]
        im_ref[t] = pltpu.roll(-(blocks[WIDTH:, :WIDTH] + blocks[:WIDTH, WIDTH:]), BAND, 1)


def place_of(number):
    point = number.astype(jnp.int32)
    grid_row = (point * 41529) >> 22
    grid_col = point - SOURCE_GRID * grid_row
    return ((grid_row * (16 * 5243)) >> 17, (grid_col * (16 * 5243)) >> 17)


def main_kernel(
    point_any,
    count_any,
    re_ref,
    im_ref,
    pupil_ref,
    row_ref,
    col_ref,
    dose_ref,
    target_ref,
    raise_ref,
    lower_ref,
    col_back_ref,
    row_back_ref,
    fold_ref,
    right_ref,
    out_ref,
    point_ref,
    count_ref,
    half_ref,
    field_ref,
    total_ref,
    slope_ref,
    back_ref,
    adj_ref,
    term_ref,
    sems,
):
    clip = lax.axis_index("clip")
    me = lax.axis_index("src")
    loads = [
        pltpu.make_async_copy(point_any, point_ref, sems.at[0]),
        pltpu.make_async_copy(count_any, count_ref, sems.at[1]),
    ]
    for load in loads:
        load.start()
    lane = lax.broadcasted_iota(jnp.int32, (BAND, WIDTH), 1)
    first_half = lane < BAND
    total_ref[...] = jnp.zeros_like(total_ref)
    adj_ref[...] = jnp.zeros_like(adj_ref)
    term_ref[...] = jnp.zeros_like(term_ref)
    rows = 2 * ROWS
    pupil_re, pupil_im = [jnp.concatenate([pupil_ref[n], pupil_ref[n]], 1) for n in range(2)]
    pupil_re_odd = jnp.where(first_half, -pupil_re, pupil_re)
    pupil_im_odd = jnp.where(first_half, -pupil_im, pupil_im)
    odd = jnp.where(first_half[:ROWS], -1.0, 1.0).astype(f32)
    for load in loads:
        load.wait()

    def weight_of(k):
        return point_ref[k >> 1, 0, 2 + (k & 1)]

    def window_of(k):
        return place_of(point_ref[k >> 1, 0, k & 1])

    def windows(step):
        for inner in range(8):
            k = step * 8 + inner
            row_pos, col_pos = window_of(k)
            inside = (lane >= col_pos) & (lane < col_pos + BAND)
            highs = []
            lows = []
            for t in range(2):
                mixed = jnp.where(
                    inside, re_ref[t, pl.ds(row_pos, BAND), :], im_ref[t, pl.ds(row_pos, BAND), :]
                )
                window = pltpu.roll(mixed, (WIDTH - col_pos) & (WIDTH - 1), 1)
                turned = pltpu.roll(mixed, (WIDTH + BAND - col_pos) & (WIDTH - 1), 1)
                high, low = split(pupil_re * window + pupil_im_odd * turned)
                highs.append(high)
                lows.append(low)
            both = mm(
                row_ref[me],
                jnp.concatenate([jnp.concatenate(highs, 1), jnp.concatenate(lows, 1)], 0),
            )
            both = both[:rows] + both[rows:]
            half = jnp.concatenate(
                [
                    both[:ROWS, at : at + WIDTH] + odd * pltpu.roll(both[ROWS:, at : at + WIDTH], BAND, 1)
                    for at in (0, WIDTH)
                ],
                0,
            )
            half_ref[pl.ds(pl.multiple_of(k * rows, rows), rows), :] = split_cols(half)

    def fields(step):
        field = mm(
            half_ref[pl.ds(pl.multiple_of(step * 8 * rows, 8 * rows), 8 * rows), :], col_ref[...]
        )
        total = total_ref[...]
        for inner in range(8):
            k = step * 8 + inner
            one = field[inner * rows : (inner + 1) * rows]
            field_ref[k] = one
            total += weight_of(k) * (
                one[:, :WIDTH] * one[:, :WIDTH] + one[:, WIDTH:] * one[:, WIDTH:]
            )
        total_ref[...] = total

    def in_turn(first, second):
        def both(step, carry):
            second(step - 1)
            first(step)
            return carry

        first(0)
        lax.fori_loop(1, POINTS // 8, both, 0)
        second(POINTS // 8 - 1)

    in_turn(windows, fields)

    intensity = mm(split_cols(total_ref[...]), raise_ref[...])
    for t in range(2):
        slot = (clip & 1) * 2 + t
        live = jnp.where(slot < count_ref[clip >> 1], 1.0, 0.0).astype(f32)
        bright = intensity[t * ROWS : (t + 1) * ROWS]
        goal = target_ref[t]
        slope = jnp.zeros((ROWS, TILE), f32)
        for s in range(DOSES):
            dose = 0.85 + 0.02 * dose_ref[t, s].astype(f32)
            printed = 1.0 / (1.0 + jnp.exp(-4.0 * (dose * bright - 1.0)))
            slope += (printed - goal) * (printed * (1.0 - printed)) * dose
        slope_ref[t * ROWS : (t + 1) * ROWS] = (8.0 * live) * slope
    slope_ref[:, :WIDTH] = mm(split_cols(slope_ref[...]), lower_ref[...])

    def columns_back(step):
        slope = slope_ref[:, :WIDTH]
        highs = []
        lows = []
        for inner in range(8):
            k = step * 8 + inner
            field = field_ref[k]
            weighed_re = slope * field[:, :WIDTH]
            weighed_im = slope * field[:, WIDTH:]
            term = jnp.sum(
                weighed_re * field[:, :WIDTH] + weighed_im * field[:, WIDTH:], 0, keepdims=True
            )
            term_ref[step * 4 + inner // 2, 2 + inner % 2 : 3 + inner % 2, :] = term
            twice = 2.0 * weight_of(k)
            high, low = split(jnp.concatenate([twice * weighed_re, twice * weighed_im], 1))
            highs.append(high)
            lows.append(low)
        half = mm(jnp.concatenate(highs, 0), col_back_ref[...])
        rest = mm(jnp.concatenate(lows, 0), col_back_ref[:, :WIDTH])
        back_ref[pl.ds(pl.multiple_of(step * 8 * rows, 8 * rows), 8 * rows), :] = (
            half[:, :WIDTH] + half[:, WIDTH:] + rest
        )

    def rows_back(step):
        for inner in range(8):
            k = step * 8 + inner
            row_pos, col_pos = window_of(k)
            inside = (lane >= col_pos) & (lane < col_pos + BAND)
            half = back_ref[pl.ds(pl.multiple_of(k * rows, rows), rows), :]
            both = mm(
                row_back_ref[me],
                split_rows(jnp.concatenate([half[:ROWS], half[ROWS:]], 1)),
            )
            for t in range(2):
                by_cos = both[:BAND, t * WIDTH : (t + 1) * WIDTH]
                by_sin = both[BAND:, t * WIDTH : (t + 1) * WIDTH]
                straight = pupil_re * by_cos - pupil_im * by_sin
                crossed = pupil_im_odd * by_cos + pupil_re_odd * by_sin
                spread = pltpu.roll(straight, col_pos, 1) + pltpu.roll(
                    crossed, (col_pos + BAND) & (WIDTH - 1), 1
                )
                adj_ref[t, pl.ds(row_pos, BAND), :] += jnp.where(inside, spread, 0.0)
                adj_ref[2 + t, pl.ds(row_pos, BAND), :] += jnp.where(inside, 0.0, spread)

    in_turn(columns_back, rows_back)

    lane = lax.broadcasted_iota(jnp.int32, (WIDTH, WIDTH), 1)
    tops = []
    bottoms = []
    top_flat = jnp.zeros((WIDTH, WIDTH), f32)
    bottom_flat = jnp.zeros((WIDTH, WIDTH), f32)
    for t in range(2):
        adj_re = adj_ref[t]
        adj_im = pltpu.roll(adj_ref[2 + t], BAND, 1)
        high, low = split(jnp.concatenate([adj_re, adj_im], 1))
        folded = mm(high, fold_ref[...]) + mm(low, fold_ref[...])
        tops.append(folded[:, :WIDTH])
        bottoms.append(folded[:, WIDTH:])
        top_flat += jnp.where(lane == t, pltpu.roll(adj_re, BAND + t, 1), 0.0)
        bottom_flat -= jnp.where(lane == t, pltpu.roll(adj_im, BAND + t, 1), 0.0)
    high, low = split(
        jnp.concatenate(
            [
                jnp.concatenate(tops + [top_flat], 1),
                jnp.concatenate(bottoms + [bottom_flat], 1),
            ],
            0,
        )
    )
    for block in range(4):
        at_rows = slice(block * WIDTH, (block + 1) * WIDTH)
        table_high = right_ref[0, at_rows, :]
        lines = mm(table_high, high) + mm(table_high, low) + mm(right_ref[1, at_rows, :], high)
        flat = lines[:, 2 * WIDTH :].T
        for n in range(4):
            owner = block * 4 + n
            own_rows = lines[n * ROWS : (n + 1) * ROWS]
            out_ref[owner, :ROWS, :] = own_rows[:, :WIDTH]
            out_ref[owner, ROWS:rows, :] = own_rows[:, WIDTH : 2 * WIDTH]
            out_ref[owner, rows:, :] = flat[:8] + term_ref[owner]


def image_kernel(chunk_ref, table_ref, out_ref, term_ref):
    me = lax.axis_index("src")
    rows = 2 * ROWS
    total = jnp.sum(chunk_ref[...], 0)
    image = mm(split_cols(total[:rows]), table_ref[...])
    last = total[rows:]
    flat = pltpu.roll(last, (WIDTH - (me & 3) * ROWS) & (WIDTH - 1), 1)
    diagonal = lax.broadcasted_iota(jnp.int32, (ROWS, WIDTH), 0) == lax.broadcasted_iota(
        jnp.int32, (ROWS, WIDTH), 1
    )
    for t in range(2):
        column = jnp.sum(jnp.where(diagonal, flat[t : t + 1], 0.0), 1, keepdims=True)
        out_ref[t] = image[t * ROWS : (t + 1) * ROWS] + column * (1.0 / math.sqrt(TILE))
    sums = jnp.sum(last, 1, keepdims=True) * (1.0 / (TILE * TILE))
    term_ref[...] = jnp.broadcast_to(jnp.broadcast_to(sums, (8, WIDTH))[None], term_ref.shape)


def per_device(
    clips, mask_field, dose_code, target, pupil, source_index, source_weight, tile_count
):
    held = {name: jnp.asarray(table) for name, table in constants().items()}
    vmem = pl.BlockSpec(memory_space=pltpu.VMEM)
    free = pl.BlockSpec(memory_space=pl.ANY)

    mine = pl.pallas_call(
        pack_kernel,
        in_specs=[free, free],
        out_shape=jax.ShapeDtypeStruct((SRC, 1, WIDTH), f32),
        scratch_shapes=[
            pltpu.SMEM(source_index.shape, jnp.int32),
            pltpu.SMEM(source_weight.shape, f32),
            pltpu.SemaphoreType.DMA((2,)),
        ],
        compiler_params=pltpu.CompilerParams(vmem_limit_bytes=2 * 1024 * 1024),
        cost_estimate=pl.CostEstimate(
            flops=8_000_000_000, bytes_accessed=20_000_000, transcendentals=0
        ),
        name="pack",
    )(source_index, source_weight)
    points = lax.all_to_all(mine, "src", 0, 0)

    spec_shape = jax.ShapeDtypeStruct((2, WIDTH, WIDTH), f32)
    spec_re, spec_im = pl.pallas_call(
        spectrum_kernel,
        in_specs=[vmem] * 3 + [free],
        out_shape=[spec_shape, spec_shape],
        compiler_params=pltpu.CompilerParams(vmem_limit_bytes=20 * 1024 * 1024),
        cost_estimate=pl.CostEstimate(
            flops=2_400_000_000, bytes_accessed=3_000_000, transcendentals=0
        ),
        name="spectrum",
    )(mask_field, held["spec_right"], held["spec_left"], mine)

    stored = [spec_re, spec_im, pupil, held["row"], held["col"]]
    stored += [dose_code, target, held["raise"], held["lower"], held["col_back"]]
    stored += [held["row_back"], held["fold"], held["spec_right"]]
    blocks = pl.pallas_call(
        main_kernel,
        in_specs=[free] * 2 + [vmem] * len(stored),
        out_shape=jax.ShapeDtypeStruct((SRC, CHUNK, WIDTH), f32),
        scratch_shapes=[
            pltpu.SMEM(points.shape, f32),
            pltpu.SMEM(tile_count.shape, jnp.int32),
            pltpu.VMEM((POINTS * 2 * ROWS, 3 * WIDTH), bf16),
            pltpu.VMEM((POINTS, 2 * ROWS, 2 * WIDTH), f32),
            pltpu.VMEM((2 * ROWS, WIDTH), f32),
            pltpu.VMEM((2 * ROWS, TILE), f32),
            pltpu.VMEM((POINTS * 2 * ROWS, WIDTH), f32),
            pltpu.VMEM((4, WIDTH, WIDTH), f32),
            pltpu.VMEM((SRC, 8, WIDTH), f32),
            pltpu.SemaphoreType.DMA((2,)),
        ],
        compiler_params=pltpu.CompilerParams(vmem_limit_bytes=28 * 1024 * 1024),
        cost_estimate=pl.CostEstimate(
            flops=8_000_000_000, bytes_accessed=5_000_000, transcendentals=300_000
        ),
        name="fields",
    )(points, tile_count, *stored)

    chunks = lax.all_to_all(blocks, "src", 0, 0)
    grad_mask, term = pl.pallas_call(
        image_kernel,
        out_shape=[
            jax.ShapeDtypeStruct((2, ROWS, TILE), f32),
            jax.ShapeDtypeStruct((clips, 8, WIDTH), f32),
        ],
        compiler_params=pltpu.CompilerParams(vmem_limit_bytes=12 * 1024 * 1024),
        cost_estimate=pl.CostEstimate(
            flops=100_000_000, bytes_accessed=1_000_000, transcendentals=0
        ),
        name="image",
    )(chunks, held["image"])
    term = lax.all_to_all(term, "clip", 0, 0)
    grad_source = jnp.sum(term[:, 2:4, 0], 0)
    return (grad_mask, grad_source)


def solution(mesh):
    return jax.shard_map(
        functools.partial(per_device, mesh.shape["clip"]),
        mesh=mesh,
        in_specs=(
            P("clip", None, None),
            P("clip", None, "src", None),
            P("clip", "src", None),
            P(),
            P("src"),
            P("src"),
            P(),
        ),
        out_specs=(P("clip", "src", None), P("src")),
        check_vma=False,
    )
```

```python
import functools
import math

import jax
import jax.numpy as jnp
import numpy as np
from jax import lax
from jax.experimental import pallas as pl
from jax.experimental.pallas import tpu as pltpu
from jax.sharding import PartitionSpec as P

SOURCE_GRID = 101
TILE = 512
BAND = 64
WIDTH = 128
SRC = 16
ROWS = TILE // SRC
DOSES = 8
POINTS = 32
CHUNK = 2 * ROWS + 8

f32 = jnp.float32
bf16 = jnp.bfloat16


def halves(table):
    whole = np.asarray(table, np.float32)
    high = whole.astype(jnp.bfloat16)
    low = (whole - high.astype(np.float32)).astype(jnp.bfloat16)
    return high, low


def as_left(table):
    high, low = halves(table)
    return np.concatenate([high, high, low], -1)


def as_right(table):
    high, low = halves(table)
    return np.concatenate([high, low, high], -2)


def angles(frequency, position):
    turns = np.outer(np.asarray(frequency), np.asarray(position)) % TILE
    return turns * (2.0 * math.pi / TILE)


@functools.cache
def constants():
    pixel = np.arange(TILE)
    coarse = np.arange(WIDTH) * (TILE // WIDTH)
    wide = np.arange(WIDTH) - BAND
    narrow = np.arange(BAND)
    held = {}
    fwd = angles(wide, pixel)
    fwd_cos = np.cos(fwd) / math.sqrt(TILE)
    fwd_sin = np.sin(fwd) / math.sqrt(TILE)
    pair = np.concatenate([fwd_cos, fwd_sin], 0)
    held["spec_right"] = np.stack(halves(pair.T))
    held["spec_left"] = np.stack(halves(pair))
    row = angles(pixel, narrow)
    row_cos = np.cos(row) / math.sqrt(BAND)
    row_sin = np.sin(row) / math.sqrt(BAND)
    lines = []
    backs = []
    for at in range(0, TILE, ROWS):
        high, low = halves(
            np.concatenate([row_cos[at : at + ROWS], row_sin[at : at + ROWS]], 0)
        )
        lines.append(
            np.concatenate(
                [np.concatenate([high, high], 1), np.concatenate([low, 0 * low], 1)], 0
            )
        )
        backs.append(
            as_left(np.concatenate([row_cos[at : at + ROWS].T, row_sin[at : at + ROWS].T], 0))
        )
    held["row"] = np.stack(lines)
    held["row_back"] = np.stack(backs)
    col = angles(narrow, coarse)
    col_cos = np.cos(col) / math.sqrt(BAND)
    col_sin = np.sin(col) / math.sqrt(BAND)
    table = np.concatenate(
        [np.concatenate([col_cos, col_sin], 1), np.concatenate([-col_sin, col_cos], 1)], 0
    )
    held["col"] = as_right(table)
    held["col_back"] = np.concatenate(halves(table.T), 1)
    gap = pixel[None, :] - coarse[:, None]
    raised = sum(np.cos((2.0 * math.pi / TILE) * (f * gap % TILE)) for f in range(1, BAND))
    raised = (1.0 + 2.0 * raised) / WIDTH
    held["raise"] = as_right(raised)
    held["lower"] = as_right(raised.T)
    order = np.arange(1, BAND + 1)
    even = (np.abs(wide)[:, None] == order).astype(np.float32)
    odd = (wide[:, None] == order).astype(np.float32) - (wide[:, None] == -order)
    none = np.zeros_like(even)
    held["fold"] = np.concatenate(
        [
            np.concatenate([even, none, none, -odd], 1),
            np.concatenate([none, -odd, -even, none], 1),
        ],
        0,
    ).astype(jnp.bfloat16)
    final = angles(order, pixel)
    held["image"] = as_right(np.concatenate([np.cos(final), np.sin(final)], 0) / math.sqrt(TILE))
    return held


def split(value):
    high = value.astype(bf16)
    low = (value - high.astype(f32)).astype(bf16)
    return high, low


def split_cols(value):
    high, low = split(value)
    return jnp.concatenate([high, high, low], 1)


def split_rows(value):
    high, low = split(value)
    return jnp.concatenate([high, low, high], 0)


def mm(left, right):
    return jnp.dot(left, right, preferred_element_type=f32)


def pack_kernel(index_ref, weight_ref, out_ref):
    lane = lax.broadcasted_iota(jnp.int32, out_ref.shape, 2)
    packed = jnp.where(lane == 0, index_ref[0], jnp.where(lane == 1, index_ref[1], 0))
    weights = jnp.where(lane == 2, weight_ref[0], jnp.where(lane == 3, weight_ref[1], 0.0))
    out_ref[...] = packed.astype(f32) + weights


def spectrum_kernel(
    mask_hbm, right_hbm, left_hbm, after_any, re_ref, im_ref, mask_ref, right_ref, left_ref, sems
):
    half_tile = TILE // 2
    pairs = [(right_hbm, right_ref)]
    for t in range(2):
        for part in range(2):
            piece = pl.ds(part * half_tile, half_tile)
            pairs.append((mask_hbm.at[t, piece], mask_ref.at[t, piece]))
    pairs.insert(3, (left_hbm, left_ref))
    loads = [pltpu.make_async_copy(*pair, sems.at[n]) for n, pair in enumerate(pairs)]
    for load in loads[:3]:
        load.start()
    for t in range(2):
        highs = []
        lows = []
        for part in range(2):
            loads[1 + 3 * t + part].wait()
            if t == 0 and part == 0:
                loads[0].wait()
                for load in loads[3:]:
                    load.start()
            high, low = split(mask_ref[t, part * half_tile : (part + 1) * half_tile])
            high, low = split(
                mm(high, right_ref[0]) + mm(high, right_ref[1]) + mm(low, right_ref[0])
            )
            highs.append(high)
            lows.append(low)
        high = jnp.concatenate(highs, 0)
        low = jnp.concatenate(lows, 0)
        if t == 0:
            loads[3].wait()
        blocks = mm(left_ref[0], high) + mm(left_ref[0], low) + mm(left_ref[1], high)
        re_ref[t] = blocks[:WIDTH, :WIDTH] - blocks[WIDTH:, WIDTH:]
        im_ref[t] = pltpu.roll(-(blocks[WIDTH:, :WIDTH] + blocks[:WIDTH, WIDTH:]), BAND, 1)


def place_of(number):
    point = number.astype(jnp.int32)
    grid_row = (point * 41529) >> 22
    grid_col = point - SOURCE_GRID * grid_row
    return ((grid_row * (16 * 5243)) >> 17, (grid_col * (16 * 5243)) >> 17)


def main_kernel(
    point_hbm,
    count_hbm,
    re_hbm,
    im_hbm,
    pupil_hbm,
    row_hbm,
    col_hbm,
    dose_hbm,
    target_hbm,
    raise_hbm,
    lower_hbm,
    col_back_hbm,
    row_back_hbm,
    fold_hbm,
    lines_hbm,
    out_ref,
    point_ref,
    count_ref,
    re_ref,
    im_ref,
    pupil_ref,
    row_ref,
    col_ref,
    dose_ref,
    target_ref,
    raise_ref,
    lower_ref,
    col_back_ref,
    row_back_ref,
    fold_ref,
    right_ref,
    half_ref,
    field_ref,
    total_ref,
    slope_ref,
    back_ref,
    adj_ref,
    term_ref,
    sems,
):
    clip = lax.axis_index("clip")
    me = lax.axis_index("src")
    loads = [
        pltpu.make_async_copy(source, target, sems.at[n])
        for n, (source, target) in enumerate(
            (
                (point_hbm, point_ref),
                (re_hbm, re_ref),
                (im_hbm, im_ref),
                (pupil_hbm, pupil_ref),
                (row_hbm.at[me], row_ref),
                (col_hbm, col_ref),
                (dose_hbm, dose_ref),
                (raise_hbm, raise_ref),
                (target_hbm, target_ref),
                (count_hbm, count_ref),
                (lower_hbm, lower_ref),
                (col_back_hbm, col_back_ref),
                (row_back_hbm.at[me], row_back_ref),
                (fold_hbm, fold_ref),
                (lines_hbm, right_ref),
            )
        )
    ]
    for load in loads:
        load.start()
    lane = lax.broadcasted_iota(jnp.int32, (BAND, WIDTH), 1)
    first_half = lane < BAND
    total_ref[...] = jnp.zeros_like(total_ref)
    adj_ref[...] = jnp.zeros_like(adj_ref)
    term_ref[...] = jnp.zeros_like(term_ref)
    rows = 2 * ROWS
    for load in loads[:6]:
        load.wait()
    pupil_re, pupil_im = [jnp.concatenate([pupil_ref[n], pupil_ref[n]], 1) for n in range(2)]
    pupil_re_odd = jnp.where(first_half, -pupil_re, pupil_re)
    pupil_im_odd = jnp.where(first_half, -pupil_im, pupil_im)
    odd = jnp.where(first_half[:ROWS], -1.0, 1.0).astype(f32)

    def weight_of(k):
        return point_ref[k >> 1, 0, 2 + (k & 1)]

    def window_of(k):
        return place_of(point_ref[k >> 1, 0, k & 1])

    def windows(step):
        for inner in range(8):
            k = step * 8 + inner
            row_pos, col_pos = window_of(k)
            inside = (lane >= col_pos) & (lane < col_pos + BAND)
            highs = []
            lows = []
            for t in range(2):
                mixed = jnp.where(
                    inside, re_ref[t, pl.ds(row_pos, BAND), :], im_ref[t, pl.ds(row_pos, BAND), :]
                )
                window = pltpu.roll(mixed, (WIDTH - col_pos) & (WIDTH - 1), 1)
                turned = pltpu.roll(mixed, (WIDTH + BAND - col_pos) & (WIDTH - 1), 1)
                high, low = split(pupil_re * window + pupil_im_odd * turned)
                highs.append(high)
                lows.append(low)
            both = mm(
                row_ref[...],
                jnp.concatenate([jnp.concatenate(highs, 1), jnp.concatenate(lows, 1)], 0),
            )
            both = both[:rows] + both[rows:]
            half = jnp.concatenate(
                [
                    both[:ROWS, at : at + WIDTH] + odd * pltpu.roll(both[ROWS:, at : at + WIDTH], BAND, 1)
                    for at in (0, WIDTH)
                ],
                0,
            )
            half_ref[pl.ds(pl.multiple_of(k * rows, rows), rows), :] = split_cols(half)

    def fields(step):
        field = mm(
            half_ref[pl.ds(pl.multiple_of(step * 8 * rows, 8 * rows), 8 * rows), :], col_ref[...]
        )
        total = total_ref[...]
        for inner in range(8):
            k = step * 8 + inner
            one = field[inner * rows : (inner + 1) * rows]
            field_ref[k] = one
            total += weight_of(k) * (
                one[:, :WIDTH] * one[:, :WIDTH] + one[:, WIDTH:] * one[:, WIDTH:]
            )
        total_ref[...] = total

    def in_turn(first, second):
        def both(step, carry):
            second(step - 1)
            first(step)
            return carry

        first(0)
        lax.fori_loop(1, POINTS // 8, both, 0)
        second(POINTS // 8 - 1)

    in_turn(windows, fields)

    for load in loads[6:]:
        load.wait()
    intensity = mm(split_cols(total_ref[...]), raise_ref[...])
    for t in range(2):
        slot = (clip & 1) * 2 + t
        live = jnp.where(slot < count_ref[clip >> 1], 1.0, 0.0).astype(f32)
        bright = intensity[t * ROWS : (t + 1) * ROWS]
        goal = target_ref[t]
        slope = jnp.zeros((ROWS, TILE), f32)
        for s in range(DOSES):
            dose = 0.85 + 0.02 * dose_ref[t, s].astype(f32)
            printed = 1.0 / (1.0 + jnp.exp(-4.0 * (dose * bright - 1.0)))
            slope += (printed - goal) * (printed * (1.0 - printed)) * dose
        slope_ref[t * ROWS : (t + 1) * ROWS] = (8.0 * live) * slope
    slope_ref[:, :WIDTH] = mm(split_cols(slope_ref[...]), lower_ref[...])

    def columns_back(step):
        slope = slope_ref[:, :WIDTH]
        highs = []
        lows = []
        for inner in range(8):
            k = step * 8 + inner
            field = field_ref[k]
            weighed_re = slope * field[:, :WIDTH]
            weighed_im = slope * field[:, WIDTH:]
            term = jnp.sum(
                weighed_re * field[:, :WIDTH] + weighed_im * field[:, WIDTH:], 0, keepdims=True
            )
            term_ref[step * 4 + inner // 2, 2 + inner % 2 : 3 + inner % 2, :] = term
            twice = 2.0 * weight_of(k)
            high, low = split(jnp.concatenate([twice * weighed_re, twice * weighed_im], 1))
            highs.append(high)
            lows.append(low)
        half = mm(jnp.concatenate(highs, 0), col_back_ref[...])
        rest = mm(jnp.concatenate(lows, 0), col_back_ref[:, :WIDTH])
        back_ref[pl.ds(pl.multiple_of(step * 8 * rows, 8 * rows), 8 * rows), :] = (
            half[:, :WIDTH] + half[:, WIDTH:] + rest
        )

    def rows_back(step):
        for inner in range(8):
            k = step * 8 + inner
            row_pos, col_pos = window_of(k)
            inside = (lane >= col_pos) & (lane < col_pos + BAND)
            half = back_ref[pl.ds(pl.multiple_of(k * rows, rows), rows), :]
            both = mm(
                row_back_ref[...],
                split_rows(jnp.concatenate([half[:ROWS], half[ROWS:]], 1)),
            )
            for t in range(2):
                by_cos = both[:BAND, t * WIDTH : (t + 1) * WIDTH]
                by_sin = both[BAND:, t * WIDTH : (t + 1) * WIDTH]
                straight = pupil_re * by_cos - pupil_im * by_sin
                crossed = pupil_im_odd * by_cos + pupil_re_odd * by_sin
                spread = pltpu.roll(straight, col_pos, 1) + pltpu.roll(
                    crossed, (col_pos + BAND) & (WIDTH - 1), 1
                )
                adj_ref[t, pl.ds(row_pos, BAND), :] += jnp.where(inside, spread, 0.0)
                adj_ref[2 + t, pl.ds(row_pos, BAND), :] += jnp.where(inside, 0.0, spread)

    in_turn(columns_back, rows_back)

    lane = lax.broadcasted_iota(jnp.int32, (WIDTH, WIDTH), 1)
    tops = []
    bottoms = []
    top_flat = jnp.zeros((WIDTH, WIDTH), f32)
    bottom_flat = jnp.zeros((WIDTH, WIDTH), f32)
    for t in range(2):
        adj_re = adj_ref[t]
        adj_im = pltpu.roll(adj_ref[2 + t], BAND, 1)
        high, low = split(jnp.concatenate([adj_re, adj_im], 1))
        folded = mm(high, fold_ref[...]) + mm(low, fold_ref[...])
        tops.append(folded[:, :WIDTH])
        bottoms.append(folded[:, WIDTH:])
        top_flat += jnp.where(lane == t, pltpu.roll(adj_re, BAND + t, 1), 0.0)
        bottom_flat -= jnp.where(lane == t, pltpu.roll(adj_im, BAND + t, 1), 0.0)
    high, low = split(
        jnp.concatenate(
            [
                jnp.concatenate(tops + [top_flat], 1),
                jnp.concatenate(bottoms + [bottom_flat], 1),
            ],
            0,
        )
    )
    for block in range(4):
        at_rows = slice(block * WIDTH, (block + 1) * WIDTH)
        table_high = right_ref[0, at_rows, :]
        lines = mm(table_high, high) + mm(table_high, low) + mm(right_ref[1, at_rows, :], high)
        flat = lines[:, 2 * WIDTH :].T
        for n in range(4):
            owner = block * 4 + n
            own_rows = lines[n * ROWS : (n + 1) * ROWS]
            out_ref[owner, :ROWS, :] = own_rows[:, :WIDTH]
            out_ref[owner, ROWS:rows, :] = own_rows[:, WIDTH : 2 * WIDTH]
            out_ref[owner, rows:, :] = flat[:8] + term_ref[owner]


def image_kernel(chunk_ref, table_ref, out_ref, term_ref):
    me = lax.axis_index("src")
    rows = 2 * ROWS
    total = jnp.sum(chunk_ref[...], 0)
    image = mm(split_cols(total[:rows]), table_ref[...])
    last = total[rows:]
    flat = pltpu.roll(last, (WIDTH - (me & 3) * ROWS) & (WIDTH - 1), 1)
    diagonal = lax.broadcasted_iota(jnp.int32, (ROWS, WIDTH), 0) == lax.broadcasted_iota(
        jnp.int32, (ROWS, WIDTH), 1
    )
    for t in range(2):
        column = jnp.sum(jnp.where(diagonal, flat[t : t + 1], 0.0), 1, keepdims=True)
        out_ref[t] = image[t * ROWS : (t + 1) * ROWS] + column * (1.0 / math.sqrt(TILE))
    sums = jnp.sum(last, 1, keepdims=True) * (1.0 / (TILE * TILE))
    term_ref[...] = jnp.broadcast_to(jnp.broadcast_to(sums, (8, WIDTH))[None], term_ref.shape)


def per_device(
    clips, mask_field, dose_code, target, pupil, source_index, source_weight, tile_count
):
    held = {name: jnp.asarray(table) for name, table in constants().items()}
    smem = pl.BlockSpec(memory_space=pltpu.SMEM)
    free = pl.BlockSpec(memory_space=pl.ANY)
    hbm = pl.BlockSpec(memory_space=pltpu.HBM)
    roomy = pltpu.CompilerParams(vmem_limit_bytes=56 * 1024 * 1024)

    mine = pl.pallas_call(
        pack_kernel,
        in_specs=[smem, smem],
        out_shape=jax.ShapeDtypeStruct((SRC, 1, WIDTH), f32),
        name="pack",
    )(source_index, source_weight)
    points = lax.all_to_all(mine, "src", 0, 0)

    stored = [mask_field, held["spec_right"], held["spec_left"]]
    spec_shape = jax.ShapeDtypeStruct((2, WIDTH, WIDTH), f32)
    spec_re, spec_im = pl.pallas_call(
        spectrum_kernel,
        in_specs=[hbm] * 3 + [free],
        out_shape=[spec_shape, spec_shape],
        scratch_shapes=[pltpu.VMEM(a.shape, a.dtype) for a in stored]
        + [pltpu.SemaphoreType.DMA((6,))],
        compiler_params=roomy,
        cost_estimate=pl.CostEstimate(
            flops=2_400_000_000, bytes_accessed=3_000_000, transcendentals=0
        ),
        name="spectrum",
    )(*stored, mine)

    stored = [points, tile_count, spec_re, spec_im, pupil, held["row"], held["col"]]
    stored += [dose_code, target, held["raise"], held["lower"], held["col_back"]]
    stored += [held["row_back"], held["fold"], held["spec_right"]]
    landing = [pltpu.VMEM(a.shape, a.dtype) for a in stored]
    landing[0] = pltpu.SMEM(points.shape, f32)
    landing[1] = pltpu.SMEM(tile_count.shape, jnp.int32)
    for n in (5, 12):
        landing[n] = pltpu.VMEM(stored[n].shape[1:], bf16)
    blocks = pl.pallas_call(
        main_kernel,
        in_specs=[free] * 4 + [hbm] * (len(stored) - 4),
        out_shape=jax.ShapeDtypeStruct((SRC, CHUNK, WIDTH), f32),
        scratch_shapes=landing
        + [
            pltpu.VMEM((POINTS * 2 * ROWS, 3 * WIDTH), bf16),
            pltpu.VMEM((POINTS, 2 * ROWS, 2 * WIDTH), f32),
            pltpu.VMEM((2 * ROWS, WIDTH), f32),
            pltpu.VMEM((2 * ROWS, TILE), f32),
            pltpu.VMEM((POINTS * 2 * ROWS, WIDTH), f32),
            pltpu.VMEM((4, WIDTH, WIDTH), f32),
            pltpu.VMEM((SRC, 8, WIDTH), f32),
            pltpu.SemaphoreType.DMA((len(stored),)),
        ],
        compiler_params=roomy,
        cost_estimate=pl.CostEstimate(
            flops=8_000_000_000, bytes_accessed=5_000_000, transcendentals=300_000
        ),
        name="fields",
    )(*stored)

    chunks = lax.all_to_all(blocks.reshape(SRC, 1, CHUNK * WIDTH), "src", 0, 0)
    chunks = chunks.reshape(SRC, CHUNK, WIDTH)
    grad_mask, term = pl.pallas_call(
        image_kernel,
        out_shape=[
            jax.ShapeDtypeStruct((2, ROWS, TILE), f32),
            jax.ShapeDtypeStruct((clips, 8, WIDTH), f32),
        ],
        compiler_params=pltpu.CompilerParams(vmem_limit_bytes=12 * 1024 * 1024),
        cost_estimate=pl.CostEstimate(
            flops=100_000_000, bytes_accessed=1_000_000, transcendentals=0
        ),
        name="image",
    )(chunks, held["image"])
    term = lax.all_to_all(term, "clip", 0, 0)
    grad_source = jnp.sum(term[:, 2:4, 0], 0)
    return (grad_mask, grad_source)


def solution(mesh):
    return jax.shard_map(
        functools.partial(per_device, mesh.shape["clip"]),
        mesh=mesh,
        in_specs=(
            P("clip", None, None),
            P("clip", None, "src", None),
            P("clip", "src", None),
            P(),
            P("src"),
            P("src"),
            P(),
        ),
        out_specs=(P("clip", "src", None), P("src")),
        check_vma=False,
    )
```

```python
import functools
import math

import jax
import jax.numpy as jnp
import numpy as np
from jax import lax
from jax.experimental import pallas as pl
from jax.experimental.pallas import tpu as pltpu
from jax.sharding import PartitionSpec as P

SOURCE_GRID = 101
TILE = 512
BAND = 64
WIDTH = 128
SRC = 16
ROWS = TILE // SRC
DOSES = 8
POINTS = 32
CHUNK = 2 * ROWS + 8

f32 = jnp.float32
bf16 = jnp.bfloat16


def halves(table):
    whole = np.asarray(table, np.float32)
    high = whole.astype(jnp.bfloat16)
    low = (whole - high.astype(np.float32)).astype(jnp.bfloat16)
    return high, low


def as_left(table):
    high, low = halves(table)
    return np.concatenate([high, high, low], -1)


def as_right(table):
    high, low = halves(table)
    return np.concatenate([high, low, high], -2)


def angles(frequency, position):
    turns = np.outer(np.asarray(frequency), np.asarray(position)) % TILE
    return turns * (2.0 * math.pi / TILE)


@functools.cache
def constants():
    pixel = np.arange(TILE)
    coarse = np.arange(WIDTH) * (TILE // WIDTH)
    wide = np.arange(WIDTH) - BAND
    narrow = np.arange(BAND)
    held = {}
    fwd = angles(wide, pixel)
    fwd_cos = np.cos(fwd) / math.sqrt(TILE)
    fwd_sin = np.sin(fwd) / math.sqrt(TILE)
    pair = np.concatenate([fwd_cos, fwd_sin], 0)
    held["spec_right"] = np.stack(halves(pair.T))
    held["spec_left"] = np.stack(halves(pair))
    row = angles(pixel, narrow)
    row_cos = np.cos(row) / math.sqrt(BAND)
    row_sin = np.sin(row) / math.sqrt(BAND)
    lines = []
    backs = []
    for at in range(0, TILE, ROWS):
        high, low = halves(
            np.concatenate([row_cos[at : at + ROWS], row_sin[at : at + ROWS]], 0)
        )
        lines.append(
            np.concatenate(
                [np.concatenate([high, high], 1), np.concatenate([low, 0 * low], 1)], 0
            )
        )
        backs.append(
            as_left(np.concatenate([row_cos[at : at + ROWS].T, row_sin[at : at + ROWS].T], 0))
        )
    held["row"] = np.stack(lines)
    held["row_back"] = np.stack(backs)
    col = angles(narrow, coarse)
    col_cos = np.cos(col) / math.sqrt(BAND)
    col_sin = np.sin(col) / math.sqrt(BAND)
    table = np.concatenate(
        [np.concatenate([col_cos, col_sin], 1), np.concatenate([-col_sin, col_cos], 1)], 0
    )
    held["col"] = as_right(table)
    held["col_back"] = np.concatenate(halves(table.T), 1)
    gap = pixel[None, :] - coarse[:, None]
    raised = sum(np.cos((2.0 * math.pi / TILE) * (f * gap % TILE)) for f in range(1, BAND))
    raised = (1.0 + 2.0 * raised) / WIDTH
    held["raise"] = as_right(raised)
    held["lower"] = as_right(raised.T)
    order = np.arange(1, BAND + 1)
    even = (np.abs(wide)[:, None] == order).astype(np.float32)
    odd = (wide[:, None] == order).astype(np.float32) - (wide[:, None] == -order)
    none = np.zeros_like(even)
    held["fold"] = np.concatenate(
        [
            np.concatenate([even, none, none, -odd], 1),
            np.concatenate([none, -odd, -even, none], 1),
        ],
        0,
    ).astype(jnp.bfloat16)
    final = angles(order, pixel)
    held["image"] = as_right(np.concatenate([np.cos(final), np.sin(final)], 0) / math.sqrt(TILE))
    return held


def split(value):
    high = value.astype(bf16)
    low = (value - high.astype(f32)).astype(bf16)
    return high, low


def split_cols(value):
    high, low = split(value)
    return jnp.concatenate([high, high, low], 1)


def split_rows(value):
    high, low = split(value)
    return jnp.concatenate([high, low, high], 0)


def mm(left, right):
    return jnp.dot(left, right, preferred_element_type=f32)


def pack_kernel(index_ref, weight_ref, out_ref):
    lane = lax.broadcasted_iota(jnp.int32, out_ref.shape, 2)
    packed = jnp.where(lane == 0, index_ref[0], jnp.where(lane == 1, index_ref[1], 0))
    weights = jnp.where(lane == 2, weight_ref[0], jnp.where(lane == 3, weight_ref[1], 0.0))
    out_ref[...] = packed.astype(f32) + weights


def spectrum_kernel(
    mask_hbm, right_hbm, left_hbm, after_any, re_ref, im_ref, mask_ref, right_ref, left_ref, sems
):
    half_tile = TILE // 2
    pairs = [(right_hbm, right_ref)]
    for t in range(2):
        for part in range(2):
            piece = pl.ds(part * half_tile, half_tile)
            pairs.append((mask_hbm.at[t, piece], mask_ref.at[t, piece]))
    pairs.insert(3, (left_hbm, left_ref))
    loads = [pltpu.make_async_copy(*pair, sems.at[n]) for n, pair in enumerate(pairs)]
    for load in loads[:3]:
        load.start()
    for t in range(2):
        highs = []
        lows = []
        for part in range(2):
            loads[1 + 3 * t + part].wait()
            if t == 0 and part == 0:
                loads[0].wait()
                for load in loads[3:]:
                    load.start()
            high, low = split(mask_ref[t, part * half_tile : (part + 1) * half_tile])
            high, low = split(
                mm(high, right_ref[0]) + mm(high, right_ref[1]) + mm(low, right_ref[0])
            )
            highs.append(high)
            lows.append(low)
        high = jnp.concatenate(highs, 0)
        low = jnp.concatenate(lows, 0)
        if t == 0:
            loads[3].wait()
        blocks = mm(left_ref[0], high) + mm(left_ref[0], low) + mm(left_ref[1], high)
        re_ref[t] = blocks[:WIDTH, :WIDTH] - blocks[WIDTH:, WIDTH:]
        im_ref[t] = pltpu.roll(-(blocks[WIDTH:, :WIDTH] + blocks[:WIDTH, WIDTH:]), BAND, 1)


def place_of(number):
    point = number.astype(jnp.int32)
    grid_row = (point * 41529) >> 22
    grid_col = point - SOURCE_GRID * grid_row
    return ((grid_row * (16 * 5243)) >> 17, (grid_col * (16 * 5243)) >> 17)


def main_kernel(
    point_hbm,
    count_hbm,
    re_hbm,
    im_hbm,
    pupil_hbm,
    row_hbm,
    col_hbm,
    dose_hbm,
    target_hbm,
    raise_hbm,
    lower_hbm,
    col_back_hbm,
    row_back_hbm,
    fold_hbm,
    lines_hbm,
    out_any,
    out_ref,
    point_ref,
    count_ref,
    re_ref,
    im_ref,
    pupil_ref,
    row_ref,
    col_ref,
    dose_ref,
    target_ref,
    raise_ref,
    lower_ref,
    col_back_ref,
    row_back_ref,
    fold_ref,
    right_ref,
    half_ref,
    field_ref,
    total_ref,
    slope_ref,
    back_ref,
    adj_ref,
    term_ref,
    sems,
):
    clip = lax.axis_index("clip")
    me = lax.axis_index("src")
    loads = [
        pltpu.make_async_copy(source, target, sems.at[n])
        for n, (source, target) in enumerate(
            (
                (point_hbm, point_ref),
                (re_hbm, re_ref),
                (im_hbm, im_ref),
                (pupil_hbm, pupil_ref),
                (row_hbm.at[me], row_ref),
                (col_hbm, col_ref),
                (dose_hbm, dose_ref),
                (raise_hbm, raise_ref),
                (target_hbm, target_ref),
                (count_hbm, count_ref),
                (lower_hbm, lower_ref),
                (col_back_hbm, col_back_ref),
                (row_back_hbm.at[me], row_back_ref),
                (fold_hbm, fold_ref),
                (lines_hbm, right_ref),
            )
        )
    ]
    for load in loads:
        load.start()
    lane = lax.broadcasted_iota(jnp.int32, (BAND, WIDTH), 1)
    first_half = lane < BAND
    total_ref[...] = jnp.zeros_like(total_ref)
    adj_ref[...] = jnp.zeros_like(adj_ref)
    term_ref[...] = jnp.zeros_like(term_ref)
    rows = 2 * ROWS
    for load in loads[:6]:
        load.wait()
    pupil_re, pupil_im = [jnp.concatenate([pupil_ref[n], pupil_ref[n]], 1) for n in range(2)]
    pupil_re_odd = jnp.where(first_half, -pupil_re, pupil_re)
    pupil_im_odd = jnp.where(first_half, -pupil_im, pupil_im)
    odd = jnp.where(first_half[:ROWS], -1.0, 1.0).astype(f32)

    def weight_of(k):
        return point_ref[k >> 1, 0, 2 + (k & 1)]

    def window_of(k):
        return place_of(point_ref[k >> 1, 0, k & 1])

    def windows(step):
        for inner in range(8):
            k = step * 8 + inner
            row_pos, col_pos = window_of(k)
            inside = (lane >= col_pos) & (lane < col_pos + BAND)
            highs = []
            lows = []
            for t in range(2):
                mixed = jnp.where(
                    inside, re_ref[t, pl.ds(row_pos, BAND), :], im_ref[t, pl.ds(row_pos, BAND), :]
                )
                window = pltpu.roll(mixed, (WIDTH - col_pos) & (WIDTH - 1), 1)
                turned = pltpu.roll(mixed, (WIDTH + BAND - col_pos) & (WIDTH - 1), 1)
                high, low = split(pupil_re * window + pupil_im_odd * turned)
                highs.append(high)
                lows.append(low)
            both = mm(
                row_ref[...],
                jnp.concatenate([jnp.concatenate(highs, 1), jnp.concatenate(lows, 1)], 0),
            )
            both = both[:rows] + both[rows:]
            half = jnp.concatenate(
                [
                    both[:ROWS, at : at + WIDTH] + odd * pltpu.roll(both[ROWS:, at : at + WIDTH], BAND, 1)
                    for at in (0, WIDTH)
                ],
                0,
            )
            half_ref[pl.ds(pl.multiple_of(k * rows, rows), rows), :] = split_cols(half)

    def fields(step):
        field = mm(
            half_ref[pl.ds(pl.multiple_of(step * 8 * rows, 8 * rows), 8 * rows), :], col_ref[...]
        )
        total = total_ref[...]
        for inner in range(8):
            k = step * 8 + inner
            one = field[inner * rows : (inner + 1) * rows]
            field_ref[k] = one
            total += weight_of(k) * (
                one[:, :WIDTH] * one[:, :WIDTH] + one[:, WIDTH:] * one[:, WIDTH:]
            )
        total_ref[...] = total

    def in_turn(first, second):
        def both(step, carry):
            second(step - 1)
            first(step)
            return carry

        first(0)
        lax.fori_loop(1, POINTS // 8, both, 0)
        second(POINTS // 8 - 1)

    in_turn(windows, fields)

    for load in loads[6:]:
        load.wait()
    intensity = mm(split_cols(total_ref[...]), raise_ref[...])
    for t in range(2):
        slot = (clip & 1) * 2 + t
        live = jnp.where(slot < count_ref[clip >> 1], 1.0, 0.0).astype(f32)
        bright = intensity[t * ROWS : (t + 1) * ROWS]
        goal = target_ref[t]
        slope = jnp.zeros((ROWS, TILE), f32)
        for s in range(DOSES):
            dose = 0.85 + 0.02 * dose_ref[t, s].astype(f32)
            printed = 1.0 / (1.0 + jnp.exp(-4.0 * (dose * bright - 1.0)))
            slope += (printed - goal) * (printed * (1.0 - printed)) * dose
        slope_ref[t * ROWS : (t + 1) * ROWS] = (8.0 * live) * slope
    slope_ref[:, :WIDTH] = mm(split_cols(slope_ref[...]), lower_ref[...])

    def columns_back(step):
        slope = slope_ref[:, :WIDTH]
        highs = []
        lows = []
        for inner in range(8):
            k = step * 8 + inner
            field = field_ref[k]
            weighed_re = slope * field[:, :WIDTH]
            weighed_im = slope * field[:, WIDTH:]
            term = jnp.sum(
                weighed_re * field[:, :WIDTH] + weighed_im * field[:, WIDTH:], 0, keepdims=True
            )
            term_ref[step * 4 + inner // 2, 2 + inner % 2 : 3 + inner % 2, :] = term
            twice = 2.0 * weight_of(k)
            high, low = split(jnp.concatenate([twice * weighed_re, twice * weighed_im], 1))
            highs.append(high)
            lows.append(low)
        half = mm(jnp.concatenate(highs, 0), col_back_ref[...])
        rest = mm(jnp.concatenate(lows, 0), col_back_ref[:, :WIDTH])
        back_ref[pl.ds(pl.multiple_of(step * 8 * rows, 8 * rows), 8 * rows), :] = (
            half[:, :WIDTH] + half[:, WIDTH:] + rest
        )

    def rows_back(step):
        for inner in range(8):
            k = step * 8 + inner
            row_pos, col_pos = window_of(k)
            inside = (lane >= col_pos) & (lane < col_pos + BAND)
            half = back_ref[pl.ds(pl.multiple_of(k * rows, rows), rows), :]
            both = mm(
                row_back_ref[...],
                split_rows(jnp.concatenate([half[:ROWS], half[ROWS:]], 1)),
            )
            for t in range(2):
                by_cos = both[:BAND, t * WIDTH : (t + 1) * WIDTH]
                by_sin = both[BAND:, t * WIDTH : (t + 1) * WIDTH]
                straight = pupil_re * by_cos - pupil_im * by_sin
                crossed = pupil_im_odd * by_cos + pupil_re_odd * by_sin
                spread = pltpu.roll(straight, col_pos, 1) + pltpu.roll(
                    crossed, (col_pos + BAND) & (WIDTH - 1), 1
                )
                adj_ref[t, pl.ds(row_pos, BAND), :] += jnp.where(inside, spread, 0.0)
                adj_ref[2 + t, pl.ds(row_pos, BAND), :] += jnp.where(inside, 0.0, spread)

    in_turn(columns_back, rows_back)

    lane = lax.broadcasted_iota(jnp.int32, (WIDTH, WIDTH), 1)
    tops = []
    bottoms = []
    top_flat = jnp.zeros((WIDTH, WIDTH), f32)
    bottom_flat = jnp.zeros((WIDTH, WIDTH), f32)
    for t in range(2):
        adj_re = adj_ref[t]
        adj_im = pltpu.roll(adj_ref[2 + t], BAND, 1)
        high, low = split(jnp.concatenate([adj_re, adj_im], 1))
        folded = mm(high, fold_ref[...]) + mm(low, fold_ref[...])
        tops.append(folded[:, :WIDTH])
        bottoms.append(folded[:, WIDTH:])
        top_flat += jnp.where(lane == t, pltpu.roll(adj_re, BAND + t, 1), 0.0)
        bottom_flat -= jnp.where(lane == t, pltpu.roll(adj_im, BAND + t, 1), 0.0)
    high, low = split(
        jnp.concatenate(
            [
                jnp.concatenate(tops + [top_flat], 1),
                jnp.concatenate(bottoms + [bottom_flat], 1),
            ],
            0,
        )
    )
    stores = []
    for block in range(4):
        at_rows = slice(block * WIDTH, (block + 1) * WIDTH)
        table_high = right_ref[0, at_rows, :]
        lines = mm(table_high, high) + mm(table_high, low) + mm(right_ref[1, at_rows, :], high)
        flat = lines[:, 2 * WIDTH :].T
        for n in range(4):
            owner = block * 4 + n
            own_rows = lines[n * ROWS : (n + 1) * ROWS]
            out_ref[owner, :ROWS, :] = own_rows[:, :WIDTH]
            out_ref[owner, ROWS:rows, :] = own_rows[:, WIDTH : 2 * WIDTH]
            out_ref[owner, rows:, :] = flat[:8] + term_ref[owner]
        owners = pl.ds(block * 4, 4)
        stores.append(
            pltpu.make_async_copy(
                out_ref.at[owners], out_any.at[owners], sems.at[len(loads) + block]
            )
        )
        stores[-1].start()
    for store in stores:
        store.wait()


def table_kernel(after_any, table_any, out_ref, sem):
    load = pltpu.make_async_copy(table_any, out_ref, sem)
    load.start()
    load.wait()


def image_kernel(chunk_ref, table_ref, out_ref, term_ref):
    me = lax.axis_index("src")
    rows = 2 * ROWS
    total = jnp.sum(chunk_ref[...], 0)
    image = mm(split_cols(total[:rows]), table_ref[...])
    last = total[rows:]
    flat = pltpu.roll(last, (WIDTH - (me & 3) * ROWS) & (WIDTH - 1), 1)
    diagonal = lax.broadcasted_iota(jnp.int32, (ROWS, WIDTH), 0) == lax.broadcasted_iota(
        jnp.int32, (ROWS, WIDTH), 1
    )
    for t in range(2):
        column = jnp.sum(jnp.where(diagonal, flat[t : t + 1], 0.0), 1, keepdims=True)
        out_ref[t] = image[t * ROWS : (t + 1) * ROWS] + column * (1.0 / math.sqrt(TILE))
    sums = jnp.sum(last, 1, keepdims=True) * (1.0 / (TILE * TILE))
    lane = lax.broadcasted_iota(jnp.int32, (1, WIDTH), 1)
    terms = jnp.where(lane == 0, sums[2:3], jnp.where(lane == 1, sums[3:4], 0.0))
    term_ref[...] = jnp.broadcast_to(terms[None], term_ref.shape)


def per_device(
    clips, mask_field, dose_code, target, pupil, source_index, source_weight, tile_count
):
    held = {name: jnp.asarray(table) for name, table in constants().items()}
    smem = pl.BlockSpec(memory_space=pltpu.SMEM)
    free = pl.BlockSpec(memory_space=pl.ANY)
    hbm = pl.BlockSpec(memory_space=pltpu.HBM)
    roomy = pltpu.CompilerParams(vmem_limit_bytes=56 * 1024 * 1024)

    mine = pl.pallas_call(
        pack_kernel,
        in_specs=[smem, smem],
        out_shape=jax.ShapeDtypeStruct((SRC, 1, WIDTH), f32),
        name="pack",
    )(source_index, source_weight)
    points = lax.all_to_all(mine, "src", 0, 0)

    stored = [mask_field, held["spec_right"], held["spec_left"]]
    spec_shape = jax.ShapeDtypeStruct((2, WIDTH, WIDTH), f32)
    spec_re, spec_im = pl.pallas_call(
        spectrum_kernel,
        in_specs=[hbm] * 3 + [free],
        out_shape=[spec_shape, spec_shape],
        scratch_shapes=[pltpu.VMEM(a.shape, a.dtype) for a in stored]
        + [pltpu.SemaphoreType.DMA((6,))],
        compiler_params=roomy,
        cost_estimate=pl.CostEstimate(
            flops=2_400_000_000, bytes_accessed=3_000_000, transcendentals=0
        ),
        name="spectrum",
    )(*stored, mine)

    stored = [points, tile_count, spec_re, spec_im, pupil, held["row"], held["col"]]
    stored += [dose_code, target, held["raise"], held["lower"], held["col_back"]]
    stored += [held["row_back"], held["fold"], held["spec_right"]]
    landing = [pltpu.VMEM(a.shape, a.dtype) for a in stored]
    landing[0] = pltpu.SMEM(points.shape, f32)
    landing[1] = pltpu.SMEM(tile_count.shape, jnp.int32)
    for n in (5, 12):
        landing[n] = pltpu.VMEM(stored[n].shape[1:], bf16)
    blocks = pl.pallas_call(
        main_kernel,
        in_specs=[free] * 4 + [hbm] * (len(stored) - 4),
        out_specs=free,
        out_shape=jax.ShapeDtypeStruct((SRC, CHUNK, WIDTH), f32),
        scratch_shapes=[pltpu.VMEM((SRC, CHUNK, WIDTH), f32)]
        + landing
        + [
            pltpu.VMEM((POINTS * 2 * ROWS, 3 * WIDTH), bf16),
            pltpu.VMEM((POINTS, 2 * ROWS, 2 * WIDTH), f32),
            pltpu.VMEM((2 * ROWS, WIDTH), f32),
            pltpu.VMEM((2 * ROWS, TILE), f32),
            pltpu.VMEM((POINTS * 2 * ROWS, WIDTH), f32),
            pltpu.VMEM((4, WIDTH, WIDTH), f32),
            pltpu.VMEM((SRC, 8, WIDTH), f32),
            pltpu.SemaphoreType.DMA((len(stored) + 4,)),
        ],
        compiler_params=roomy,
        cost_estimate=pl.CostEstimate(
            flops=8_000_000_000, bytes_accessed=5_000_000, transcendentals=300_000
        ),
        name="fields",
    )(*stored)

    chunks = lax.all_to_all(blocks.reshape(SRC, 1, CHUNK * WIDTH), "src", 0, 0)
    chunks = chunks.reshape(SRC, CHUNK, WIDTH)
    small = pltpu.CompilerParams(vmem_limit_bytes=12 * 1024 * 1024)
    table = pl.pallas_call(
        table_kernel,
        in_specs=[free, free],
        out_shape=jax.ShapeDtypeStruct(held["image"].shape, bf16),
        scratch_shapes=[pltpu.SemaphoreType.DMA],
        compiler_params=small,
        cost_estimate=pl.CostEstimate(flops=0, bytes_accessed=800_000, transcendentals=0),
        name="table",
    )(blocks, held["image"])
    grad_mask, term = pl.pallas_call(
        image_kernel,
        out_shape=[
            jax.ShapeDtypeStruct((2, ROWS, TILE), f32),
            jax.ShapeDtypeStruct((clips, 1, WIDTH), f32),
        ],
        compiler_params=small,
        cost_estimate=pl.CostEstimate(
            flops=100_000_000, bytes_accessed=1_000_000, transcendentals=0
        ),
        name="image",
    )(chunks, table)
    term = lax.all_to_all(term, "clip", 0, 0)
    grad_source = jnp.sum(term[:, 0, :2], 0)
    return (grad_mask, grad_source)


def solution(mesh):
    return jax.shard_map(
        functools.partial(per_device, mesh.shape["clip"]),
        mesh=mesh,
        in_specs=(
            P("clip", None, None),
            P("clip", None, "src", None),
            P("clip", "src", None),
            P(),
            P("src"),
            P("src"),
            P(),
        ),
        out_specs=(P("clip", "src", None), P("src")),
        check_vma=False,
    )
```

```python
import functools
import math

import jax
import jax.numpy as jnp
import numpy as np
from jax import lax
from jax.experimental import pallas as pl
from jax.experimental.pallas import tpu as pltpu
from jax.sharding import PartitionSpec as P

SOURCE_GRID = 101
TILE = 512
BAND = 64
WIDTH = 128
SRC = 16
ROWS = TILE // SRC
DOSES = 8
POINTS = 32
CHUNK = 2 * ROWS + 1

f32 = jnp.float32
bf16 = jnp.bfloat16


def halves(table):
    whole = np.asarray(table, np.float32)
    high = whole.astype(jnp.bfloat16)
    low = (whole - high.astype(np.float32)).astype(jnp.bfloat16)
    return high, low


def as_left(table):
    high, low = halves(table)
    return np.concatenate([high, high, low], -1)


def as_right(table):
    high, low = halves(table)
    return np.concatenate([high, low, high], -2)


def angles(frequency, position):
    turns = np.outer(np.asarray(frequency), np.asarray(position)) % TILE
    return turns * (2.0 * math.pi / TILE)


@functools.cache
def constants():
    pixel = np.arange(TILE)
    coarse = np.arange(WIDTH) * (TILE // WIDTH)
    wide = np.arange(WIDTH) - BAND
    narrow = np.arange(BAND)
    held = {}
    fwd = angles(wide, pixel)
    fwd_cos = np.cos(fwd) / math.sqrt(TILE)
    fwd_sin = np.sin(fwd) / math.sqrt(TILE)
    pair = np.concatenate([fwd_cos, fwd_sin], 0)
    held["spec_right"] = np.stack(halves(pair.T))
    held["spec_left"] = np.stack(halves(pair))
    row = angles(pixel, narrow)
    row_cos = np.cos(row) / math.sqrt(BAND)
    row_sin = np.sin(row) / math.sqrt(BAND)
    lines = []
    backs = []
    for at in range(0, TILE, ROWS):
        high, low = halves(
            np.concatenate([row_cos[at : at + ROWS], row_sin[at : at + ROWS]], 0)
        )
        lines.append(
            np.concatenate(
                [np.concatenate([high, high], 1), np.concatenate([low, 0 * low], 1)], 0
            )
        )
        backs.append(
            as_left(np.concatenate([row_cos[at : at + ROWS].T, row_sin[at : at + ROWS].T], 0))
        )
    held["row"] = np.stack(lines)
    held["row_back"] = np.stack(backs)
    col = angles(narrow, coarse)
    col_cos = np.cos(col) / math.sqrt(BAND)
    col_sin = np.sin(col) / math.sqrt(BAND)
    table = np.concatenate(
        [np.concatenate([col_cos, col_sin], 1), np.concatenate([-col_sin, col_cos], 1)], 0
    )
    held["col"] = as_right(table)
    held["col_back"] = np.concatenate(halves(table.T), 1)
    gap = pixel[None, :] - coarse[:, None]
    raised = sum(np.cos((2.0 * math.pi / TILE) * (f * gap % TILE)) for f in range(1, BAND))
    raised = (1.0 + 2.0 * raised) / WIDTH
    held["raise"] = as_right(raised)
    held["lower"] = as_right(raised.T)
    order = np.arange(1, BAND + 1)
    even = (np.abs(wide)[:, None] == order).astype(np.float32)
    odd = (wide[:, None] == order).astype(np.float32) - (wide[:, None] == -order)
    none = np.zeros_like(even)
    held["fold"] = np.concatenate(
        [
            np.concatenate([even, none, none, -odd], 1),
            np.concatenate([none, -odd, -even, none], 1),
        ],
        0,
    ).astype(jnp.bfloat16)
    final = angles(order, pixel)
    held["image"] = as_right(np.concatenate([np.cos(final), np.sin(final)], 0) / math.sqrt(TILE))
    return held


def split(value):
    high = value.astype(bf16)
    low = (value - high.astype(f32)).astype(bf16)
    return high, low


def split_cols(value):
    high, low = split(value)
    return jnp.concatenate([high, high, low], 1)


def split_rows(value):
    high, low = split(value)
    return jnp.concatenate([high, low, high], 0)


def mm(left, right):
    return jnp.dot(left, right, preferred_element_type=f32)


def pack_kernel(index_ref, weight_ref, out_ref):
    lane = lax.broadcasted_iota(jnp.int32, out_ref.shape, 2)
    packed = jnp.where(lane == 0, index_ref[0], jnp.where(lane == 1, index_ref[1], 0))
    weights = jnp.where(lane == 2, weight_ref[0], jnp.where(lane == 3, weight_ref[1], 0.0))
    out_ref[...] = packed.astype(f32) + weights


def spectrum_kernel(
    mask_hbm,
    right_hbm,
    left_hbm,
    after_any,
    re_any,
    im_any,
    mask_ref,
    right_ref,
    left_ref,
    re_ref,
    im_ref,
    sems,
):
    pieces = [(0, 0, 256), (0, 256, 256), (1, 0, 256), (1, 256, 128), (1, 384, 128)]
    pairs = [
        (mask_hbm.at[t, pl.ds(at, size)], mask_ref.at[t, pl.ds(at, size)])
        for t, at, size in pieces
    ]
    pairs += [(right_hbm, right_ref), (left_hbm, left_ref)]
    loads = [pltpu.make_async_copy(*pair, sems.at[n]) for n, pair in enumerate(pairs)]
    for n in (5, 0, 1, 6, 2, 3, 4):
        loads[n].start()
    loads[5].wait()
    stores = []
    for t in range(2):
        highs = []
        lows = []
        for n, (tile, at, size) in enumerate(pieces):
            if tile != t:
                continue
            loads[n].wait()
            high, low = split(mask_ref[t, at : at + size])
            high, low = split(
                mm(high, right_ref[0]) + mm(high, right_ref[1]) + mm(low, right_ref[0])
            )
            highs.append(high)
            lows.append(low)
        high = jnp.concatenate(highs, 0)
        low = jnp.concatenate(lows, 0)
        if t == 0:
            loads[6].wait()
        blocks = mm(left_ref[0], high) + mm(left_ref[0], low) + mm(left_ref[1], high)
        re_ref[t] = blocks[:WIDTH, :WIDTH] - blocks[WIDTH:, WIDTH:]
        im_ref[t] = pltpu.roll(-(blocks[WIDTH:, :WIDTH] + blocks[:WIDTH, WIDTH:]), BAND, 1)
        for n, (source, target) in enumerate(((re_ref, re_any), (im_ref, im_any))):
            stores.append(
                pltpu.make_async_copy(source.at[t], target.at[t], sems.at[7 + 2 * t + n])
            )
            stores[-1].start()
    for store in stores:
        store.wait()


def place_of(number):
    point = number.astype(jnp.int32)
    grid_row = (point * 41529) >> 22
    grid_col = point - SOURCE_GRID * grid_row
    return ((grid_row * (16 * 5243)) >> 17, (grid_col * (16 * 5243)) >> 17)


def main_kernel(
    point_hbm,
    count_hbm,
    re_hbm,
    im_hbm,
    pupil_hbm,
    row_hbm,
    col_hbm,
    dose_hbm,
    target_hbm,
    raise_hbm,
    lower_hbm,
    col_back_hbm,
    row_back_hbm,
    fold_hbm,
    lines_hbm,
    out_any,
    out_ref,
    point_ref,
    count_ref,
    re_ref,
    im_ref,
    pupil_ref,
    row_ref,
    col_ref,
    dose_ref,
    target_ref,
    raise_ref,
    lower_ref,
    col_back_ref,
    row_back_ref,
    fold_ref,
    right_ref,
    half_ref,
    field_ref,
    total_ref,
    slope_ref,
    back_ref,
    adj_ref,
    term_ref,
    sems,
):
    clip = lax.axis_index("clip")
    me = lax.axis_index("src")
    loads = [
        pltpu.make_async_copy(source, target, sems.at[n])
        for n, (source, target) in enumerate(
            (
                (point_hbm, point_ref),
                (re_hbm, re_ref),
                (im_hbm, im_ref),
                (pupil_hbm, pupil_ref),
                (row_hbm.at[me], row_ref),
                (col_hbm, col_ref),
                (dose_hbm, dose_ref),
                (raise_hbm, raise_ref),
                (target_hbm, target_ref),
                (count_hbm, count_ref),
                (lower_hbm, lower_ref),
                (col_back_hbm, col_back_ref),
                (row_back_hbm.at[me], row_back_ref),
                (fold_hbm, fold_ref),
                (lines_hbm, right_ref),
            )
        )
    ]
    for load in loads:
        load.start()
    lane = lax.broadcasted_iota(jnp.int32, (BAND, WIDTH), 1)
    first_half = lane < BAND
    total_ref[...] = jnp.zeros_like(total_ref)
    adj_ref[...] = jnp.zeros_like(adj_ref)
    term_ref[...] = jnp.zeros_like(term_ref)
    rows = 2 * ROWS
    for load in loads[:6]:
        load.wait()
    pupil_re, pupil_im = [jnp.concatenate([pupil_ref[n], pupil_ref[n]], 1) for n in range(2)]
    pupil_re_odd = jnp.where(first_half, -pupil_re, pupil_re)
    pupil_im_odd = jnp.where(first_half, -pupil_im, pupil_im)
    odd = jnp.where(first_half[:ROWS], -1.0, 1.0).astype(f32)

    def weight_of(k):
        return point_ref[k >> 1, 0, 2 + (k & 1)]

    def window_of(k):
        return place_of(point_ref[k >> 1, 0, k & 1])

    def windows(step):
        for inner in range(8):
            k = step * 8 + inner
            row_pos, col_pos = window_of(k)
            inside = (lane >= col_pos) & (lane < col_pos + BAND)
            highs = []
            lows = []
            for t in range(2):
                mixed = jnp.where(
                    inside, re_ref[t, pl.ds(row_pos, BAND), :], im_ref[t, pl.ds(row_pos, BAND), :]
                )
                window = pltpu.roll(mixed, (WIDTH - col_pos) & (WIDTH - 1), 1)
                turned = pltpu.roll(mixed, (WIDTH + BAND - col_pos) & (WIDTH - 1), 1)
                high, low = split(pupil_re * window + pupil_im_odd * turned)
                highs.append(high)
                lows.append(low)
            both = mm(
                row_ref[...],
                jnp.concatenate([jnp.concatenate(highs, 1), jnp.concatenate(lows, 1)], 0),
            )
            both = both[:rows] + both[rows:]
            half = jnp.concatenate(
                [
                    both[:ROWS, at : at + WIDTH] + odd * pltpu.roll(both[ROWS:, at : at + WIDTH], BAND, 1)
                    for at in (0, WIDTH)
                ],
                0,
            )
            half_ref[pl.ds(pl.multiple_of(k * rows, rows), rows), :] = split_cols(half)

    def fields(step):
        field = mm(
            half_ref[pl.ds(pl.multiple_of(step * 8 * rows, 8 * rows), 8 * rows), :], col_ref[...]
        )
        total = total_ref[...]
        for inner in range(8):
            k = step * 8 + inner
            one = field[inner * rows : (inner + 1) * rows]
            field_ref[k] = one
            total += weight_of(k) * (
                one[:, :WIDTH] * one[:, :WIDTH] + one[:, WIDTH:] * one[:, WIDTH:]
            )
        total_ref[...] = total

    def in_turn(first, second):
        def both(step, carry):
            second(step - 1)
            first(step)
            return carry

        first(0)
        lax.fori_loop(1, POINTS // 8, both, 0)
        second(POINTS // 8 - 1)

    in_turn(windows, fields)

    for load in loads[6:]:
        load.wait()
    intensity = mm(split_cols(total_ref[...]), raise_ref[...])
    for t in range(2):
        slot = (clip & 1) * 2 + t
        live = jnp.where(slot < count_ref[clip >> 1], 1.0, 0.0).astype(f32)
        bright = intensity[t * ROWS : (t + 1) * ROWS]
        goal = target_ref[t]
        slope = jnp.zeros((ROWS, TILE), f32)
        for s in range(DOSES):
            dose = 0.85 + 0.02 * dose_ref[t, s].astype(f32)
            printed = 1.0 / (1.0 + jnp.exp(-4.0 * (dose * bright - 1.0)))
            slope += (printed - goal) * (printed * (1.0 - printed)) * dose
        slope_ref[t * ROWS : (t + 1) * ROWS] = (8.0 * live) * slope
    slope_ref[:, :WIDTH] = mm(split_cols(slope_ref[...]), lower_ref[...])

    def columns_back(step):
        slope = slope_ref[:, :WIDTH]
        highs = []
        lows = []
        for inner in range(8):
            k = step * 8 + inner
            field = field_ref[k]
            weighed_re = slope * field[:, :WIDTH]
            weighed_im = slope * field[:, WIDTH:]
            term = jnp.sum(
                weighed_re * field[:, :WIDTH] + weighed_im * field[:, WIDTH:], 0, keepdims=True
            )
            term_ref[step * 4 + inner // 2, 2 + inner % 2 : 3 + inner % 2, :] = term
            twice = 2.0 * weight_of(k)
            high, low = split(jnp.concatenate([twice * weighed_re, twice * weighed_im], 1))
            highs.append(high)
            lows.append(low)
        half = mm(jnp.concatenate(highs, 0), col_back_ref[...])
        rest = mm(jnp.concatenate(lows, 0), col_back_ref[:, :WIDTH])
        back_ref[pl.ds(pl.multiple_of(step * 8 * rows, 8 * rows), 8 * rows), :] = (
            half[:, :WIDTH] + half[:, WIDTH:] + rest
        )

    def rows_back(step):
        for inner in range(8):
            k = step * 8 + inner
            row_pos, col_pos = window_of(k)
            inside = (lane >= col_pos) & (lane < col_pos + BAND)
            half = back_ref[pl.ds(pl.multiple_of(k * rows, rows), rows), :]
            both = mm(
                row_back_ref[...],
                split_rows(jnp.concatenate([half[:ROWS], half[ROWS:]], 1)),
            )
            for t in range(2):
                by_cos = both[:BAND, t * WIDTH : (t + 1) * WIDTH]
                by_sin = both[BAND:, t * WIDTH : (t + 1) * WIDTH]
                straight = pupil_re * by_cos - pupil_im * by_sin
                crossed = pupil_im_odd * by_cos + pupil_re_odd * by_sin
                spread = pltpu.roll(straight, col_pos, 1) + pltpu.roll(
                    crossed, (col_pos + BAND) & (WIDTH - 1), 1
                )
                adj_ref[t, pl.ds(row_pos, BAND), :] += jnp.where(inside, spread, 0.0)
                adj_ref[2 + t, pl.ds(row_pos, BAND), :] += jnp.where(inside, 0.0, spread)

    in_turn(columns_back, rows_back)

    lane = lax.broadcasted_iota(jnp.int32, (WIDTH, WIDTH), 1)
    tops = []
    bottoms = []
    top_flat = jnp.zeros((WIDTH, WIDTH), f32)
    bottom_flat = jnp.zeros((WIDTH, WIDTH), f32)
    for t in range(2):
        adj_re = adj_ref[t]
        adj_im = pltpu.roll(adj_ref[2 + t], BAND, 1)
        high, low = split(jnp.concatenate([adj_re, adj_im], 1))
        folded = mm(high, fold_ref[...]) + mm(low, fold_ref[...])
        tops.append(folded[:, :WIDTH])
        bottoms.append(folded[:, WIDTH:])
        top_flat += jnp.where(lane == t, pltpu.roll(adj_re, BAND + t, 1), 0.0)
        bottom_flat -= jnp.where(lane == t, pltpu.roll(adj_im, BAND + t, 1), 0.0)
    high, low = split(
        jnp.concatenate(
            [
                jnp.concatenate(tops + [top_flat], 1),
                jnp.concatenate(bottoms + [bottom_flat], 1),
            ],
            0,
        )
    )
    stores = []
    place = lane[:1]
    for block in range(4):
        at_rows = slice(block * WIDTH, (block + 1) * WIDTH)
        table_high = right_ref[0, at_rows, :]
        lines = mm(table_high, high) + mm(table_high, low) + mm(right_ref[1, at_rows, :], high)
        flat = lines[:, 2 * WIDTH :].T
        for n in range(4):
            owner = block * 4 + n
            base = owner * CHUNK
            own_rows = lines[n * ROWS : (n + 1) * ROWS]
            out_ref[base : base + ROWS, :] = own_rows[:, :WIDTH]
            out_ref[base + ROWS : base + rows, :] = own_rows[:, WIDTH : 2 * WIDTH]
            sums = jnp.sum(term_ref[owner], 1, keepdims=True)
            line = jnp.where(place == rows, sums[2:3], jnp.where(place == rows + 1, sums[3:4], 0.0))
            for t in (1, 0):
                turned = pltpu.roll(flat[t : t + 1], (WIDTH + (t - n) * ROWS) % WIDTH, 1)
                line = jnp.where(place < (t + 1) * ROWS, turned, line)
            out_ref[base + rows : base + CHUNK, :] = line
        if block % 2:
            owners = pl.ds((block - 1) * 4 * CHUNK, 8 * CHUNK)
            stores.append(
                pltpu.make_async_copy(
                    out_ref.at[owners], out_any.at[owners], sems.at[len(loads) + block // 2]
                )
            )
            stores[-1].start()
    for store in stores:
        store.wait()


def table_kernel(after_any, table_any, out_ref, sem):
    load = pltpu.make_async_copy(table_any, out_ref, sem)
    load.start()
    load.wait()


def image_kernel(chunk_ref, table_ref, out_ref, term_ref):
    rows = 2 * ROWS
    total = chunk_ref[:rows]
    last = chunk_ref[rows:CHUNK]
    for n in range(1, SRC):
        total += chunk_ref[n * CHUNK : n * CHUNK + rows]
        last += chunk_ref[n * CHUNK + rows : (n + 1) * CHUNK]
    image = mm(split_cols(total), table_ref[...])
    row = lax.broadcasted_iota(jnp.int32, (ROWS, WIDTH), 0)
    lane = lax.broadcasted_iota(jnp.int32, (ROWS, WIDTH), 1)
    for t in range(2):
        column = jnp.sum(jnp.where(lane == row + t * ROWS, last, 0.0), 1, keepdims=True)
        out_ref[t] = image[t * ROWS : (t + 1) * ROWS] + column * (1.0 / math.sqrt(TILE))
    terms = jnp.where(lane[:1] < 2, pltpu.roll(last, WIDTH - rows, 1), 0.0) * (1.0 / (TILE * TILE))
    term_ref[...] = jnp.broadcast_to(terms[None], term_ref.shape)


def per_device(
    clips, mask_field, dose_code, target, pupil, source_index, source_weight, tile_count
):
    held = {name: jnp.asarray(table) for name, table in constants().items()}
    smem = pl.BlockSpec(memory_space=pltpu.SMEM)
    free = pl.BlockSpec(memory_space=pl.ANY)
    hbm = pl.BlockSpec(memory_space=pltpu.HBM)
    roomy = pltpu.CompilerParams(vmem_limit_bytes=56 * 1024 * 1024)

    mine = pl.pallas_call(
        pack_kernel,
        in_specs=[smem, smem],
        out_shape=jax.ShapeDtypeStruct((SRC, 1, WIDTH), f32),
        name="pack",
    )(source_index, source_weight)
    points = lax.all_to_all(mine, "src", 0, 0)

    stored = [mask_field, held["spec_right"], held["spec_left"]]
    spec_shape = jax.ShapeDtypeStruct((2, WIDTH, WIDTH), f32)
    spec_re, spec_im = pl.pallas_call(
        spectrum_kernel,
        in_specs=[hbm] * 3 + [free],
        out_specs=[free, free],
        out_shape=[spec_shape, spec_shape],
        scratch_shapes=[pltpu.VMEM(a.shape, a.dtype) for a in stored]
        + [pltpu.VMEM(spec_shape.shape, f32)] * 2
        + [pltpu.SemaphoreType.DMA((11,))],
        compiler_params=roomy,
        cost_estimate=pl.CostEstimate(
            flops=2_400_000_000, bytes_accessed=3_000_000, transcendentals=0
        ),
        name="spectrum",
    )(*stored, mine)

    stored = [points, tile_count, spec_re, spec_im, pupil, held["row"], held["col"]]
    stored += [dose_code, target, held["raise"], held["lower"], held["col_back"]]
    stored += [held["row_back"], held["fold"], held["spec_right"]]
    landing = [pltpu.VMEM(a.shape, a.dtype) for a in stored]
    landing[0] = pltpu.SMEM(points.shape, f32)
    landing[1] = pltpu.SMEM(tile_count.shape, jnp.int32)
    for n in (5, 12):
        landing[n] = pltpu.VMEM(stored[n].shape[1:], bf16)
    blocks = pl.pallas_call(
        main_kernel,
        in_specs=[free] * 4 + [hbm] * (len(stored) - 4),
        out_specs=free,
        out_shape=jax.ShapeDtypeStruct((SRC * CHUNK, WIDTH), f32),
        scratch_shapes=[pltpu.VMEM((SRC * CHUNK, WIDTH), f32)]
        + landing
        + [
            pltpu.VMEM((POINTS * 2 * ROWS, 3 * WIDTH), bf16),
            pltpu.VMEM((POINTS, 2 * ROWS, 2 * WIDTH), f32),
            pltpu.VMEM((2 * ROWS, WIDTH), f32),
            pltpu.VMEM((2 * ROWS, TILE), f32),
            pltpu.VMEM((POINTS * 2 * ROWS, WIDTH), f32),
            pltpu.VMEM((4, WIDTH, WIDTH), f32),
            pltpu.VMEM((SRC, 8, WIDTH), f32),
            pltpu.SemaphoreType.DMA((len(stored) + 4,)),
        ],
        compiler_params=roomy,
        cost_estimate=pl.CostEstimate(
            flops=8_000_000_000, bytes_accessed=5_000_000, transcendentals=300_000
        ),
        name="fields",
    )(*stored)

    chunks = lax.all_to_all(blocks.reshape(SRC, 1, CHUNK * WIDTH), "src", 0, 0)
    chunks = chunks.reshape(SRC * CHUNK, WIDTH)
    small = pltpu.CompilerParams(vmem_limit_bytes=12 * 1024 * 1024)
    table = pl.pallas_call(
        table_kernel,
        in_specs=[free, free],
        out_shape=jax.ShapeDtypeStruct(held["image"].shape, bf16),
        scratch_shapes=[pltpu.SemaphoreType.DMA],
        compiler_params=small,
        cost_estimate=pl.CostEstimate(flops=0, bytes_accessed=800_000, transcendentals=0),
        name="table",
    )(blocks, held["image"])
    grad_mask, term = pl.pallas_call(
        image_kernel,
        out_shape=[
            jax.ShapeDtypeStruct((2, ROWS, TILE), f32),
            jax.ShapeDtypeStruct((clips, 1, WIDTH), f32),
        ],
        compiler_params=small,
        cost_estimate=pl.CostEstimate(
            flops=100_000_000, bytes_accessed=1_000_000, transcendentals=0
        ),
        name="image",
    )(chunks, table)
    term = lax.all_to_all(term, "clip", 0, 0)
    grad_source = jnp.sum(term[:, 0, :2], 0)
    return (grad_mask, grad_source)


def solution(mesh):
    return jax.shard_map(
        functools.partial(per_device, mesh.shape["clip"]),
        mesh=mesh,
        in_specs=(
            P("clip", None, None),
            P("clip", None, "src", None),
            P("clip", "src", None),
            P(),
            P("src"),
            P("src"),
            P(),
        ),
        out_specs=(P("clip", "src", None), P("src")),
        check_vma=False,
    )
```

```python
import functools
import math

import jax
import jax.numpy as jnp
import numpy as np
from jax import lax
from jax.experimental import pallas as pl
from jax.experimental.pallas import tpu as pltpu
from jax.sharding import PartitionSpec as P

SOURCE_GRID = 101
TILE = 512
BAND = 64
WIDTH = 128
SRC = 16
ROWS = TILE // SRC
DOSES = 8
POINTS = 32
CHUNK = 2 * ROWS + 1

f32 = jnp.float32
bf16 = jnp.bfloat16


def halves(table):
    whole = np.asarray(table, np.float32)
    high = whole.astype(jnp.bfloat16)
    low = (whole - high.astype(np.float32)).astype(jnp.bfloat16)
    return high, low


def as_left(table):
    high, low = halves(table)
    return np.concatenate([high, high, low], -1)


def as_right(table):
    high, low = halves(table)
    return np.concatenate([high, low, high], -2)


def angles(frequency, position):
    turns = np.outer(np.asarray(frequency), np.asarray(position)) % TILE
    return turns * (2.0 * math.pi / TILE)


@functools.cache
def constants():
    pixel = np.arange(TILE)
    coarse = np.arange(WIDTH) * (TILE // WIDTH)
    wide = np.arange(WIDTH) - BAND
    narrow = np.arange(BAND)
    held = {}
    fwd = angles(wide, pixel)
    fwd_cos = np.cos(fwd) / math.sqrt(TILE)
    fwd_sin = np.sin(fwd) / math.sqrt(TILE)
    pair = np.concatenate([fwd_cos, fwd_sin], 0)
    held["spec_right"] = np.stack(halves(pair.T))
    held["spec_left"] = np.stack(halves(pair))
    row = angles(pixel, narrow)
    row_cos = np.cos(row) / math.sqrt(BAND)
    row_sin = np.sin(row) / math.sqrt(BAND)
    lines = []
    backs = []
    for at in range(0, TILE, ROWS):
        high, low = halves(
            np.concatenate([row_cos[at : at + ROWS], row_sin[at : at + ROWS]], 0)
        )
        lines.append(
            np.concatenate(
                [np.concatenate([high, high], 1), np.concatenate([low, 0 * low], 1)], 0
            )
        )
        backs.append(
            as_left(np.concatenate([row_cos[at : at + ROWS].T, row_sin[at : at + ROWS].T], 0))
        )
    held["row"] = np.stack(lines)
    held["row_back"] = np.stack(backs)
    col = angles(narrow, coarse)
    col_cos = np.cos(col) / math.sqrt(BAND)
    col_sin = np.sin(col) / math.sqrt(BAND)
    table = np.concatenate(
        [np.concatenate([col_cos, col_sin], 1), np.concatenate([-col_sin, col_cos], 1)], 0
    )
    held["col"] = as_right(table)
    held["col_back"] = np.concatenate(halves(table.T), 1)
    gap = pixel[None, :] - coarse[:, None]
    raised = sum(np.cos((2.0 * math.pi / TILE) * (f * gap % TILE)) for f in range(1, BAND))
    raised = (1.0 + 2.0 * raised) / WIDTH
    held["raise"] = as_right(raised)
    held["lower"] = as_right(raised.T)
    order = np.arange(1, BAND + 1)
    even = (np.abs(wide)[:, None] == order).astype(np.float32)
    odd = (wide[:, None] == order).astype(np.float32) - (wide[:, None] == -order)
    none = np.zeros_like(even)
    held["fold"] = np.concatenate(
        [
            np.concatenate([even, none, none, -odd], 1),
            np.concatenate([none, -odd, -even, none], 1),
        ],
        0,
    ).astype(jnp.bfloat16)
    final = angles(order, pixel)
    held["image"] = as_right(np.concatenate([np.cos(final), np.sin(final)], 0) / math.sqrt(TILE))
    return held


def split(value):
    high = value.astype(bf16)
    low = (value - high.astype(f32)).astype(bf16)
    return high, low


def split_cols(value):
    high, low = split(value)
    return jnp.concatenate([high, high, low], 1)


def split_rows(value):
    high, low = split(value)
    return jnp.concatenate([high, low, high], 0)


def mm(left, right):
    return jnp.dot(left, right, preferred_element_type=f32)


def pack_kernel(index_ref, weight_ref, out_ref):
    lane = lax.broadcasted_iota(jnp.int32, out_ref.shape, 2)
    packed = jnp.where(lane == 0, index_ref[0], jnp.where(lane == 1, index_ref[1], 0))
    weights = jnp.where(lane == 2, weight_ref[0], jnp.where(lane == 3, weight_ref[1], 0.0))
    out_ref[...] = packed.astype(f32) + weights


def spectrum_kernel(
    mask_hbm,
    right_hbm,
    left_hbm,
    after_any,
    re_any,
    im_any,
    mask_ref,
    right_ref,
    left_ref,
    re_ref,
    im_ref,
    sems,
):
    pieces = [(0, 0, 256), (0, 256, 256), (1, 0, 256), (1, 256, 128), (1, 384, 128)]
    pairs = [
        (mask_hbm.at[t, pl.ds(at, size)], mask_ref.at[t, pl.ds(at, size)])
        for t, at, size in pieces
    ]
    pairs += [(right_hbm, right_ref), (left_hbm, left_ref)]
    loads = [pltpu.make_async_copy(*pair, sems.at[n]) for n, pair in enumerate(pairs)]
    for n in (5, 0, 1, 6, 2, 3, 4):
        loads[n].start()
    loads[5].wait()
    stores = []
    for t in range(2):
        highs = []
        lows = []
        for n, (tile, at, size) in enumerate(pieces):
            if tile != t:
                continue
            loads[n].wait()
            high, low = split(mask_ref[t, at : at + size])
            high, low = split(
                mm(high, right_ref[0]) + mm(high, right_ref[1]) + mm(low, right_ref[0])
            )
            highs.append(high)
            lows.append(low)
        high = jnp.concatenate(highs, 0)
        low = jnp.concatenate(lows, 0)
        if t == 0:
            loads[6].wait()
        blocks = mm(left_ref[0], high) + mm(left_ref[0], low) + mm(left_ref[1], high)
        re_ref[t] = blocks[:WIDTH, :WIDTH] - blocks[WIDTH:, WIDTH:]
        im_ref[t] = pltpu.roll(-(blocks[WIDTH:, :WIDTH] + blocks[:WIDTH, WIDTH:]), BAND, 1)
        for n, (source, target) in enumerate(((re_ref, re_any), (im_ref, im_any))):
            stores.append(
                pltpu.make_async_copy(source.at[t], target.at[t], sems.at[7 + 2 * t + n])
            )
            stores[-1].start()
    for store in stores:
        store.wait()


def place_of(number):
    point = number.astype(jnp.int32)
    grid_row = (point * 41529) >> 22
    grid_col = point - SOURCE_GRID * grid_row
    return ((grid_row * (16 * 5243)) >> 17, (grid_col * (16 * 5243)) >> 17)


def main_kernel(
    point_hbm,
    count_hbm,
    re_hbm,
    im_hbm,
    pupil_hbm,
    row_hbm,
    col_hbm,
    dose_hbm,
    target_hbm,
    raise_hbm,
    lower_hbm,
    col_back_hbm,
    row_back_hbm,
    fold_hbm,
    lines_hbm,
    out_any,
    out_ref,
    point_ref,
    count_ref,
    re_ref,
    im_ref,
    pupil_ref,
    row_ref,
    col_ref,
    dose_ref,
    target_ref,
    raise_ref,
    lower_ref,
    col_back_ref,
    row_back_ref,
    fold_ref,
    right_ref,
    half_ref,
    field_ref,
    total_ref,
    slope_ref,
    back_ref,
    adj_ref,
    term_ref,
    sems,
):
    clip = lax.axis_index("clip")
    me = lax.axis_index("src")
    loads = [
        pltpu.make_async_copy(source, target, sems.at[n])
        for n, (source, target) in enumerate(
            (
                (point_hbm, point_ref),
                (re_hbm, re_ref),
                (im_hbm, im_ref),
                (pupil_hbm, pupil_ref),
                (row_hbm.at[me], row_ref),
                (col_hbm, col_ref),
                (dose_hbm, dose_ref),
                (raise_hbm, raise_ref),
                (target_hbm, target_ref),
                (count_hbm, count_ref),
                (lower_hbm, lower_ref),
                (col_back_hbm, col_back_ref),
                (row_back_hbm.at[me], row_back_ref),
                (fold_hbm, fold_ref),
                (lines_hbm, right_ref),
            )
        )
    ]
    for load in loads[:6]:
        load.start()
    lane = lax.broadcasted_iota(jnp.int32, (BAND, WIDTH), 1)
    first_half = lane < BAND
    total_ref[...] = jnp.zeros_like(total_ref)
    adj_ref[...] = jnp.zeros_like(adj_ref)
    term_ref[...] = jnp.zeros_like(term_ref)
    rows = 2 * ROWS
    for load in loads[:6]:
        load.wait()
    for load in loads[6:]:
        load.start()
    pupil_re, pupil_im = [jnp.concatenate([pupil_ref[n], pupil_ref[n]], 1) for n in range(2)]
    pupil_re_odd = jnp.where(first_half, -pupil_re, pupil_re)
    pupil_im_odd = jnp.where(first_half, -pupil_im, pupil_im)
    odd = jnp.where(first_half[:ROWS], -1.0, 1.0).astype(f32)

    def weight_of(k):
        return point_ref[k >> 1, 0, 2 + (k & 1)]

    def window_of(k):
        return place_of(point_ref[k >> 1, 0, k & 1])

    def windows(step):
        for inner in range(8):
            k = step * 8 + inner
            row_pos, col_pos = window_of(k)
            inside = (lane >= col_pos) & (lane < col_pos + BAND)
            highs = []
            lows = []
            for t in range(2):
                mixed = jnp.where(
                    inside, re_ref[t, pl.ds(row_pos, BAND), :], im_ref[t, pl.ds(row_pos, BAND), :]
                )
                window = pltpu.roll(mixed, (WIDTH - col_pos) & (WIDTH - 1), 1)
                turned = pltpu.roll(mixed, (WIDTH + BAND - col_pos) & (WIDTH - 1), 1)
                high, low = split(pupil_re * window + pupil_im_odd * turned)
                highs.append(high)
                lows.append(low)
            both = mm(
                row_ref[...],
                jnp.concatenate([jnp.concatenate(highs, 1), jnp.concatenate(lows, 1)], 0),
            )
            both = both[:rows] + both[rows:]
            half = jnp.concatenate(
                [
                    both[:ROWS, at : at + WIDTH] + odd * pltpu.roll(both[ROWS:, at : at + WIDTH], BAND, 1)
                    for at in (0, WIDTH)
                ],
                0,
            )
            half_ref[pl.ds(pl.multiple_of(k * rows, rows), rows), :] = split_cols(half)

    def fields(step):
        field = mm(
            half_ref[pl.ds(pl.multiple_of(step * 8 * rows, 8 * rows), 8 * rows), :], col_ref[...]
        )
        total = total_ref[...]
        for inner in range(8):
            k = step * 8 + inner
            one = field[inner * rows : (inner + 1) * rows]
            field_ref[k] = one
            total += weight_of(k) * (
                one[:, :WIDTH] * one[:, :WIDTH] + one[:, WIDTH:] * one[:, WIDTH:]
            )
        total_ref[...] = total

    def in_turn(first, second):
        def both(step, carry):
            second(step - 1)
            first(step)
            return carry

        first(0)
        lax.fori_loop(1, POINTS // 8, both, 0)
        second(POINTS // 8 - 1)

    in_turn(windows, fields)

    for load in loads[6:]:
        load.wait()
    intensity = mm(split_cols(total_ref[...]), raise_ref[...])
    for t in range(2):
        slot = (clip & 1) * 2 + t
        live = jnp.where(slot < count_ref[clip >> 1], 1.0, 0.0).astype(f32)
        bright = intensity[t * ROWS : (t + 1) * ROWS]
        goal = target_ref[t]
        slope = jnp.zeros((ROWS, TILE), f32)
        for s in range(DOSES):
            dose = 0.85 + 0.02 * dose_ref[t, s].astype(f32)
            printed = 1.0 / (1.0 + jnp.exp(-4.0 * (dose * bright - 1.0)))
            slope += (printed - goal) * (printed * (1.0 - printed)) * dose
        slope_ref[t * ROWS : (t + 1) * ROWS] = (8.0 * live) * slope
    slope_ref[:, :WIDTH] = mm(split_cols(slope_ref[...]), lower_ref[...])

    def columns_back(step):
        slope = slope_ref[:, :WIDTH]
        highs = []
        lows = []
        for inner in range(8):
            k = step * 8 + inner
            field = field_ref[k]
            weighed_re = slope * field[:, :WIDTH]
            weighed_im = slope * field[:, WIDTH:]
            term = jnp.sum(
                weighed_re * field[:, :WIDTH] + weighed_im * field[:, WIDTH:], 0, keepdims=True
            )
            term_ref[step * 4 + inner // 2, 2 + inner % 2 : 3 + inner % 2, :] = term
            twice = 2.0 * weight_of(k)
            high, low = split(jnp.concatenate([twice * weighed_re, twice * weighed_im], 1))
            highs.append(high)
            lows.append(low)
        half = mm(jnp.concatenate(highs, 0), col_back_ref[...])
        rest = mm(jnp.concatenate(lows, 0), col_back_ref[:, :WIDTH])
        back_ref[pl.ds(pl.multiple_of(step * 8 * rows, 8 * rows), 8 * rows), :] = (
            half[:, :WIDTH] + half[:, WIDTH:] + rest
        )

    def rows_back(step):
        for inner in range(8):
            k = step * 8 + inner
            row_pos, col_pos = window_of(k)
            inside = (lane >= col_pos) & (lane < col_pos + BAND)
            half = back_ref[pl.ds(pl.multiple_of(k * rows, rows), rows), :]
            both = mm(
                row_back_ref[...],
                split_rows(jnp.concatenate([half[:ROWS], half[ROWS:]], 1)),
            )
            for t in range(2):
                by_cos = both[:BAND, t * WIDTH : (t + 1) * WIDTH]
                by_sin = both[BAND:, t * WIDTH : (t + 1) * WIDTH]
                straight = pupil_re * by_cos - pupil_im * by_sin
                crossed = pupil_im_odd * by_cos + pupil_re_odd * by_sin
                spread = pltpu.roll(straight, col_pos, 1) + pltpu.roll(
                    crossed, (col_pos + BAND) & (WIDTH - 1), 1
                )
                adj_ref[t, pl.ds(row_pos, BAND), :] += jnp.where(inside, spread, 0.0)
                adj_ref[2 + t, pl.ds(row_pos, BAND), :] += jnp.where(inside, 0.0, spread)

    in_turn(columns_back, rows_back)

    lane = lax.broadcasted_iota(jnp.int32, (WIDTH, WIDTH), 1)
    tops = []
    bottoms = []
    top_flat = jnp.zeros((WIDTH, WIDTH), f32)
    bottom_flat = jnp.zeros((WIDTH, WIDTH), f32)
    for t in range(2):
        adj_re = adj_ref[t]
        adj_im = pltpu.roll(adj_ref[2 + t], BAND, 1)
        high, low = split(jnp.concatenate([adj_re, adj_im], 1))
        folded = mm(high, fold_ref[...]) + mm(low, fold_ref[...])
        tops.append(folded[:, :WIDTH])
        bottoms.append(folded[:, WIDTH:])
        top_flat += jnp.where(lane == t, pltpu.roll(adj_re, BAND + t, 1), 0.0)
        bottom_flat -= jnp.where(lane == t, pltpu.roll(adj_im, BAND + t, 1), 0.0)
    high, low = split(
        jnp.concatenate(
            [
                jnp.concatenate(tops + [top_flat], 1),
                jnp.concatenate(bottoms + [bottom_flat], 1),
            ],
            0,
        )
    )
    stores = []
    place = lane[:1]
    for block in range(4):
        at_rows = slice(block * WIDTH, (block + 1) * WIDTH)
        table_high = right_ref[0, at_rows, :]
        lines = mm(table_high, high) + mm(table_high, low) + mm(right_ref[1, at_rows, :], high)
        flat = lines[:, 2 * WIDTH :].T
        for n in range(4):
            owner = block * 4 + n
            base = owner * CHUNK
            own_rows = lines[n * ROWS : (n + 1) * ROWS]
            out_ref[base : base + ROWS, :] = own_rows[:, :WIDTH]
            out_ref[base + ROWS : base + rows, :] = own_rows[:, WIDTH : 2 * WIDTH]
            sums = jnp.sum(term_ref[owner], 1, keepdims=True)
            line = jnp.where(place == rows, sums[2:3], jnp.where(place == rows + 1, sums[3:4], 0.0))
            for t in (1, 0):
                turned = pltpu.roll(flat[t : t + 1], (WIDTH + (t - n) * ROWS) % WIDTH, 1)
                line = jnp.where(place < (t + 1) * ROWS, turned, line)
            out_ref[base + rows : base + CHUNK, :] = line
        if block % 2:
            owners = pl.ds((block - 1) * 4 * CHUNK, 8 * CHUNK)
            stores.append(
                pltpu.make_async_copy(
                    out_ref.at[owners], out_any.at[owners], sems.at[len(loads) + block // 2]
                )
            )
            stores[-1].start()
    for store in stores:
        store.wait()


def table_kernel(after_any, table_any, out_ref, sem):
    load = pltpu.make_async_copy(table_any, out_ref, sem)
    load.start()
    load.wait()


def image_kernel(chunk_ref, table_ref, out_ref, term_ref):
    rows = 2 * ROWS
    total = chunk_ref[:rows]
    last = chunk_ref[rows:CHUNK]
    for n in range(1, SRC):
        total += chunk_ref[n * CHUNK : n * CHUNK + rows]
        last += chunk_ref[n * CHUNK + rows : (n + 1) * CHUNK]
    image = mm(split_cols(total), table_ref[...])
    row = lax.broadcasted_iota(jnp.int32, (ROWS, WIDTH), 0)
    lane = lax.broadcasted_iota(jnp.int32, (ROWS, WIDTH), 1)
    for t in range(2):
        column = jnp.sum(jnp.where(lane == row + t * ROWS, last, 0.0), 1, keepdims=True)
        out_ref[t] = image[t * ROWS : (t + 1) * ROWS] + column * (1.0 / math.sqrt(TILE))
    terms = jnp.where(lane[:1] < 2, pltpu.roll(last, WIDTH - rows, 1), 0.0) * (1.0 / (TILE * TILE))
    term_ref[...] = jnp.broadcast_to(terms[None], term_ref.shape)


def per_device(
    clips, mask_field, dose_code, target, pupil, source_index, source_weight, tile_count
):
    held = {name: jnp.asarray(table) for name, table in constants().items()}
    smem = pl.BlockSpec(memory_space=pltpu.SMEM)
    free = pl.BlockSpec(memory_space=pl.ANY)
    hbm = pl.BlockSpec(memory_space=pltpu.HBM)
    roomy = pltpu.CompilerParams(vmem_limit_bytes=56 * 1024 * 1024)

    mine = pl.pallas_call(
        pack_kernel,
        in_specs=[smem, smem],
        out_shape=jax.ShapeDtypeStruct((SRC, 1, WIDTH), f32),
        name="pack",
    )(source_index, source_weight)
    points = lax.all_to_all(mine, "src", 0, 0)

    stored = [mask_field, held["spec_right"], held["spec_left"]]
    spec_shape = jax.ShapeDtypeStruct((2, WIDTH, WIDTH), f32)
    spec_re, spec_im = pl.pallas_call(
        spectrum_kernel,
        in_specs=[hbm] * 3 + [free],
        out_specs=[free, free],
        out_shape=[spec_shape, spec_shape],
        scratch_shapes=[pltpu.VMEM(a.shape, a.dtype) for a in stored]
        + [pltpu.VMEM(spec_shape.shape, f32)] * 2
        + [pltpu.SemaphoreType.DMA((11,))],
        compiler_params=roomy,
        cost_estimate=pl.CostEstimate(
            flops=2_400_000_000, bytes_accessed=3_000_000, transcendentals=0
        ),
        name="spectrum",
    )(*stored, mine)

    stored = [points, tile_count, spec_re, spec_im, pupil, held["row"], held["col"]]
    stored += [dose_code, target, held["raise"], held["lower"], held["col_back"]]
    stored += [held["row_back"], held["fold"], held["spec_right"]]
    landing = [pltpu.VMEM(a.shape, a.dtype) for a in stored]
    landing[0] = pltpu.SMEM(points.shape, f32)
    landing[1] = pltpu.SMEM(tile_count.shape, jnp.int32)
    for n in (5, 12):
        landing[n] = pltpu.VMEM(stored[n].shape[1:], bf16)
    blocks = pl.pallas_call(
        main_kernel,
        in_specs=[free] * 4 + [hbm] * (len(stored) - 4),
        out_specs=free,
        out_shape=jax.ShapeDtypeStruct((SRC * CHUNK, WIDTH), f32),
        scratch_shapes=[pltpu.VMEM((SRC * CHUNK, WIDTH), f32)]
        + landing
        + [
            pltpu.VMEM((POINTS * 2 * ROWS, 3 * WIDTH), bf16),
            pltpu.VMEM((POINTS, 2 * ROWS, 2 * WIDTH), f32),
            pltpu.VMEM((2 * ROWS, WIDTH), f32),
            pltpu.VMEM((2 * ROWS, TILE), f32),
            pltpu.VMEM((POINTS * 2 * ROWS, WIDTH), f32),
            pltpu.VMEM((4, WIDTH, WIDTH), f32),
            pltpu.VMEM((SRC, 8, WIDTH), f32),
            pltpu.SemaphoreType.DMA((len(stored) + 4,)),
        ],
        compiler_params=roomy,
        cost_estimate=pl.CostEstimate(
            flops=8_000_000_000, bytes_accessed=5_000_000, transcendentals=300_000
        ),
        name="fields",
    )(*stored)

    chunks = lax.all_to_all(blocks.reshape(SRC, 1, CHUNK * WIDTH), "src", 0, 0)
    chunks = chunks.reshape(SRC * CHUNK, WIDTH)
    small = pltpu.CompilerParams(vmem_limit_bytes=12 * 1024 * 1024)
    table = pl.pallas_call(
        table_kernel,
        in_specs=[free, free],
        out_shape=jax.ShapeDtypeStruct(held["image"].shape, bf16),
        scratch_shapes=[pltpu.SemaphoreType.DMA],
        compiler_params=small,
        cost_estimate=pl.CostEstimate(flops=0, bytes_accessed=800_000, transcendentals=0),
        name="table",
    )(blocks, held["image"])
    grad_mask, term = pl.pallas_call(
        image_kernel,
        out_shape=[
            jax.ShapeDtypeStruct((2, ROWS, TILE), f32),
            jax.ShapeDtypeStruct((clips, 1, WIDTH), f32),
        ],
        compiler_params=small,
        cost_estimate=pl.CostEstimate(
            flops=100_000_000, bytes_accessed=1_000_000, transcendentals=0
        ),
        name="image",
    )(chunks, table)
    term = lax.all_to_all(term, "clip", 0, 0)
    grad_source = jnp.sum(term[:, 0, :2], 0)
    return (grad_mask, grad_source)


def solution(mesh):
    return jax.shard_map(
        functools.partial(per_device, mesh.shape["clip"]),
        mesh=mesh,
        in_specs=(
            P("clip", None, None),
            P("clip", None, "src", None),
            P("clip", "src", None),
            P(),
            P("src"),
            P("src"),
            P(),
        ),
        out_specs=(P("clip", "src", None), P("src")),
        check_vma=False,
    )
```
